512 devices in a mesh: member: 16 (over z_hi, x), band: 32 (over z_lo, y, core).
Axes of the slice: x: 4, y: 8, z: 8 (z_hi: 4, z_lo: 2; z = z_hi * 2 + z_lo), core: 2. Of those that a mesh axis runs over, the one named last changes fastest.
Arguments:
- queries: bfloat16 [131072, 1024], P(('member', 'band')), parts along dimension 0, may hold values from -5 to 5
- keys: bfloat16 [131072, 1024], P(('member', 'band')), parts along dimension 0, may hold values from -5 to 5
- values: bfloat16 [131072, 1024], P(('member', 'band')), parts along dimension 0, may hold values from -5 to 5
- out_grad: bfloat16 [131072, 1024], P(('member', 'band')), parts along dimension 0, may hold values from -5 to 5
- band_counts: int32 [512], P(('member', 'band')), parts along dimension 0, may hold values from 192 to 256, as said below
- block_lists: int32 [4096, 14], P(('member', 'band')), parts along dimension 0, may hold values from 0 to 19, as said below
- slot_counts: int32 [4096], P(('member', 'band')), parts along dimension 0, may hold values from 7 to 14, as said below
Outputs:
- query_grad: bfloat16 [131072, 1024], P(('member', 'band')), parts along dimension 0
- key_grad: bfloat16 [131072, 1024], P(('member', 'band')), parts along dimension 0
- value_grad: bfloat16 [131072, 1024], P(('member', 'band')), parts along dimension 0
The draws below stay inside these ranges and needn't reach their ends.
There are 16 independent parts, one for each index of `member`. The reference program is written for one: setup_inputs(seed, part) draws one part's arguments, and reference() takes and returns one part's arrays. A program takes and returns all parts, laid end to end along the dimension named above; each array names one. Nothing has to cross between parts.
Inputs may be any that keep to these rules, and one draw needn't show every extreme that they name: `band_counts`: a band's valid tokens are its first rows; every band has at least the 192 rows that neighbours read, the middle band all of its rows, the first band exactly 192. `block_lists`: entry (b * 8 + n, l) names a frame block of band b: 0 to 7 the band's own blocks, 8 + r block r of band b - 1, 14 + r block r of band b + 1; slot 0 names block n itself; the live slots are distinct and never name a band below the first or above the last; slots past the live ones may name any frame block. `slot_counts`: some block of every band other than the first and last has all 14 slots live.
All inputs are finite; a program needn't handle non-finite values.
Results may differ from the reference program's by a relative error of at most 0.0093.
Values may be sent and summed in bfloat16 or wider, within the bound.
No kernel may reach another device: no remote copies, remote signals or barrier semaphores. Data moves between devices by JAX's collectives and lax.ppermute only.
A program may use at most 64 MiB of HBM per device.

```python
import jax
import jax.numpy as jnp
from jax import lax

HEADS = 8
HD = 128
BLK = 32
NB = 8
RB = 6
SLOTS = 14
WIDTH = 1024
BANDS = 32
BLOCKS = 256
TOKENS = 8192


def draw_queries(key, part):
    key = jax.random.fold_in(key, 1)
    base = jnp.clip(jax.random.normal(key, (TOKENS, HEADS * HD), jnp.float32), -5.0, 5.0)
    return base.astype(jnp.bfloat16)


def draw_keys(key, part):
    key = jax.random.fold_in(key, 2)
    base = jnp.clip(jax.random.normal(key, (TOKENS, HEADS * HD), jnp.float32), -5.0, 5.0)
    return base.astype(jnp.bfloat16)


def draw_band_counts(key, part):
    key = jax.random.fold_in(key, 3)
    tok = NB * BLK
    rim = RB * BLK
    half = BANDS // 2
    band = jnp.arange(BANDS, dtype=jnp.int32)
    dist = jnp.abs(band - half)
    jitter = jax.random.randint(key, (BANDS,), 0, BLK) * (dist > 0).astype(jnp.int32)
    count = tok - (tok - rim) * dist // half - jitter
    return jnp.maximum(count, rim).astype(jnp.int32)


def list_tables(key):
    key = jax.random.fold_in(key, 5)
    key_score, key_live, key_pick = jax.random.split(key, 3)
    frame_blocks = NB + 2 * RB
    block = jnp.arange(BLOCKS, dtype=jnp.int32)
    band = block // NB
    own = block % NB
    slot = jnp.arange(frame_blocks, dtype=jnp.int32)[None, :]
    usable = (slot < NB) | (slot < NB + RB) & (band[:, None] > 0) | (slot >= NB + RB) & (band[:, None] < BANDS - 1)
    score = jax.random.randint(key_score, (BLOCKS, frame_blocks), 0, 2 ** 20) * frame_blocks + slot
    score = jnp.where(slot == own[:, None], 2 ** 28, score)
    score = jnp.where(usable, score, -1 - slot)
    order = jnp.argsort(-score, axis=1, stable=True)[:, :SLOTS]
    live = jax.random.randint(key_live, (BLOCKS,), (SLOTS + 1) // 2, SLOTS + 1)
    pick = jax.random.randint(key_pick, (BANDS,), 0, NB)
    live = jnp.where(own == pick[band], SLOTS, live)
    live = jnp.minimum(live, jnp.sum(usable.astype(jnp.int32), axis=1))
    return (order.astype(jnp.int32), live.astype(jnp.int32))


def draw_block_lists(key, part):
    return list_tables(key)[0]


def draw_slot_counts(key, part):
    return list_tables(key)[1]


def shard_levels(rng, shape, cuts, least, top_value):
    factor_of, own = 1.0, jax.random.fold_in(rng, 6)
    for axis_at, parts in cuts:
        draws = jnp.exp(jax.random.uniform(jax.random.fold_in(own, axis_at), (parts,), jnp.float32, least / len(cuts), top_value / len(cuts)))
        factor_of = factor_of * jnp.repeat(draws, shape[axis_at] // parts).reshape([-1 if axis == axis_at else 1 for axis in range(len(shape))])
    return factor_of


def normal_values(stream_key, extent, scale, bound, cuts=(), kind=jnp.bfloat16):
    factor_of = shard_levels(stream_key, extent, cuts, -0.22, 0.18) if cuts else 1.0
    result = jax.random.normal(stream_key, extent, jnp.float32) * scale * factor_of
    return jnp.minimum(jnp.maximum(result, -bound), bound).astype(kind)


def setup_inputs(seed: int = 0, part: int = 0) -> dict:
    key_list = jax.random.split(jax.random.key(seed), 8)
    own_keys = jax.random.split(jax.random.fold_in(key_list[7], part), 8)
    queries = draw_queries(jax.random.fold_in(jax.random.fold_in(key_list[7], part), 71), part)
    keys = draw_keys(jax.random.fold_in(jax.random.fold_in(key_list[7], part), 71), part)
    values = normal_values(own_keys[2], (TOKENS, WIDTH), 1.0, 5.0, ((0, 32),))
    out_grad = normal_values(own_keys[3], (TOKENS, WIDTH), 1.0, 5.0, ((0, 32),))
    band_counts = draw_band_counts(jax.random.fold_in(jax.random.fold_in(key_list[7], part), 71), part)
    block_lists = draw_block_lists(jax.random.fold_in(jax.random.fold_in(key_list[7], part), 71), part)
    slot_counts = draw_slot_counts(jax.random.fold_in(jax.random.fold_in(key_list[7], part), 71), part)
    return {"queries": queries, "keys": keys, "values": values, "out_grad": out_grad, "band_counts": band_counts, "block_lists": block_lists, "slot_counts": slot_counts}


def reference(queries, keys, values, out_grad, band_counts, block_lists, slot_counts):
    tok = NB * BLK
    rim = RB * BLK
    frame_blocks = NB + 2 * RB
    width = HEADS * HD
    scale = HD ** -0.5
    q_all = queries.reshape(BANDS, tok, width)
    k_all = keys.reshape(BANDS, tok, width)
    v_all = values.reshape(BANDS, tok, width)
    g_all = out_grad.reshape(BANDS, tok, width)
    lists = block_lists.reshape(BANDS, NB, SLOTS)
    lives = slot_counts.reshape(BANDS, NB)

    def frame_of(stacked, band):
        below = stacked[jnp.maximum(band - 1, 0), :rim]
        above = stacked[jnp.minimum(band + 1, BANDS - 1), :rim]
        below = jnp.where(band > 0, below, jnp.zeros_like(below))
        above = jnp.where(band < BANDS - 1, above, jnp.zeros_like(above))
        return jnp.concatenate([stacked[band], below, above], axis=0)

    def per_band(band):
        count = band_counts[band]
        frame_k = frame_of(k_all, band)
        frame_v = frame_of(v_all, band)
        list_b = lists[band]
        live_b = lives[band]
        rows = jnp.arange(frame_blocks * BLK, dtype=jnp.int32)
        key_valid = ((rows < count) | (rows >= tok)).reshape(frame_blocks, BLK)
        slot_live = jnp.arange(SLOTS, dtype=jnp.int32)[None, :] < live_b[:, None]
        key_mask = (slot_live[:, :, None] & key_valid[list_b]).reshape(NB, SLOTS * BLK)
        query_mask = jnp.arange(tok, dtype=jnp.int32).reshape(NB, BLK) < count
        allowed = (query_mask[:, :, None] & key_mask[:, None, :])[:, None]
        k_cols = frame_k.reshape(frame_blocks, BLK, HEADS, HD)[list_b].reshape(NB, SLOTS * BLK, HEADS, HD).astype(jnp.float32)
        v_cols = frame_v.reshape(frame_blocks, BLK, HEADS, HD)[list_b].reshape(NB, SLOTS * BLK, HEADS, HD).astype(jnp.float32)
        q_b = q_all[band].reshape(NB, BLK, HEADS, HD).astype(jnp.float32)
        g_b = g_all[band].reshape(NB, BLK, HEADS, HD).astype(jnp.float32)
        score = jnp.einsum('nqhd,nkhd->nhqk', q_b, k_cols) * scale
        masked = jnp.where(allowed, score, -1e30)
        top = jnp.max(masked, axis=-1, keepdims=True)
        total = jnp.sum(jnp.where(allowed, jnp.exp(masked - top), 0.0), axis=-1, keepdims=True)
        total = total + jnp.where(jnp.any(allowed, axis=-1, keepdims=True), 0.0, 1.0)
        lse = top + jnp.log(total)
        weight = jnp.where(allowed, jnp.exp(masked - lse), 0.0)
        weight_b = weight.astype(jnp.bfloat16).astype(jnp.float32)
        attended = jnp.einsum('nhqk,nkhd->nqhd', weight_b, v_cols)
        delta = jnp.sum(g_b * attended, axis=-1).transpose(0, 2, 1)
        product = jnp.einsum('nqhd,nkhd->nhqk', g_b, v_cols)
        score_grad = (scale * weight * (product - delta[..., None])).astype(jnp.bfloat16).astype(jnp.float32)
        grad_q = jnp.einsum('nhqk,nkhd->nqhd', score_grad, k_cols)
        grad_k = jnp.einsum('nhqk,nqhd->nkhd', score_grad, q_b).reshape(NB, SLOTS, BLK, width)
        grad_v = jnp.einsum('nhqk,nqhd->nkhd', weight_b, g_b).reshape(NB, SLOTS, BLK, width)
        selector = (list_b[:, :, None] == jnp.arange(frame_blocks, dtype=jnp.int32)).astype(jnp.float32)
        frame_gk = jnp.einsum('nle,nlbf->ebf', selector, grad_k, precision=lax.Precision.HIGHEST)
        frame_gv = jnp.einsum('nle,nlbf->ebf', selector, grad_v, precision=lax.Precision.HIGHEST)
        return (grad_q.reshape(tok, width), frame_gk.reshape(frame_blocks * BLK, width),
                frame_gv.reshape(frame_blocks * BLK, width))

    grad_q, frames_k, frames_v = lax.map(per_band, jnp.arange(BANDS, dtype=jnp.int32))

    def assemble(frames):
        own = frames[:, :tok]
        empty = jnp.zeros((1, rim, width), jnp.float32)
        from_above = jnp.concatenate([frames[1:, tok:tok + rim], empty], axis=0)
        from_below = jnp.concatenate([empty, frames[:-1, tok + rim:]], axis=0)
        leading = own[:, :rim] + from_above + from_below
        return jnp.concatenate([leading, own[:, rim:]], axis=1).reshape(TOKENS, width).astype(jnp.bfloat16)

    return grad_q.reshape(TOKENS, width).astype(jnp.bfloat16), assemble(frames_k), assemble(frames_v)
```

```python
import functools
import jax
import jax.numpy as jnp
from jax import lax
from jax.experimental import pallas as pl
from jax.experimental.pallas import tpu as pltpu
from jax.sharding import PartitionSpec as P

HEADS = 8
DEPTH = 128
BLK = 32
RB = 6
RIM = RB * BLK
TABLE = 32
LOG2E = 1.4426950408889634
NEG = -1e30
FLOOR = -1e20
MIB = 1024 * 1024
LOAD_LIMIT = 51.2
GATHER = True
SPLIT = 4


def nt(a, b):
    return lax.dot_general(a, b, (((1,), (1,)), ((), ())), preferred_element_type=jnp.float32)


def tn(a, b):
    return lax.dot_general(a, b, (((0,), (0,)), ((), ())), preferred_element_type=jnp.float32)


def nn(a, b):
    return jnp.dot(a, b, preferred_element_type=jnp.float32)


def cols(h):
    return slice(h * DEPTH, (h + 1) * DEPTH)


def biased(score, bias, first):
    scaled = score * (DEPTH ** -0.5 * LOG2E)
    parts = [
        scaled[at * BLK : (at + 1) * BLK] + bias[first + at : first + at + 1, :]
        for at in range(score.shape[0] // BLK)
    ]
    return jnp.concatenate(parts, axis=0)


def table_of(lists, live, ids, count, tok):
    blocks, slots = lists.shape
    hit = jnp.zeros((blocks, ids.shape[1]), jnp.float32)
    for l in range(slots):
        hit = jnp.where((lists[:, l : l + 1] == ids) & (live > l), 1.0, hit)
    lane = lax.broadcasted_iota(jnp.int32, (blocks, tok), 1)
    row = lax.broadcasted_iota(jnp.int32, (blocks, tok), 0)
    spread = jnp.where((lane // BLK == row) & (lane < count), 1.0, 0.0)
    return jnp.where(tn(hit, spread) > 0.5, 0.0, NEG)


def own_score(k, q, bias):
    x = nt(k, q) * (DEPTH ** -0.5 * LOG2E)
    parts = [x[at * BLK : (at + 1) * BLK] + bias[at : at + 1, :] for at in range(RB)]
    return jnp.concatenate(parts + [x[RIM:] + bias[TABLE:, :]], axis=0)


def stats_of(x, prod):
    top = jnp.maximum(jnp.max(x, axis=0, keepdims=True), FLOOR)
    p = jnp.exp2(x - top)
    return top, jnp.sum(p, axis=0, keepdims=True), jnp.sum(p * prod, axis=0, keepdims=True)


def merged(a, b):
    top = jnp.maximum(a[0], b[0])
    fa, fb = jnp.exp2(a[0] - top), jnp.exp2(b[0] - top)
    return top, a[1] * fa + b[1] * fb, a[2] * fa + b[2] * fb


def grads_of(x, prod, top, inv, delta):
    p = jnp.exp2(x - top)
    w = (p * inv).astype(jnp.bfloat16)
    ds = (p * (inv * (DEPTH ** -0.5)) * (prod - delta)).astype(jnp.bfloat16)
    return w, ds


def swap_across(x):
    count = lax.axis_size("band")
    pairs = [(at, at + 1) for at in range(1, count - 1, 2)]
    return lax.ppermute(x, "band", pairs + [(b, a) for a, b in pairs])


def swap_inside(x):
    if not GATHER:
        return lax.ppermute(x, "band", [(at, at ^ 1) for at in range(lax.axis_size("band"))])
    pairs = [[at, at + 1] for at in range(0, lax.axis_size("band"), 2)]
    return lax.all_gather(x, "band", axis_index_groups=pairs)


def load_kernel(
    k_ref, v_ref, q_ref, g_ref, lead_ref, k_out, v_out, q_out, g_out, sems
):
    tok = k_ref.shape[0]
    lead = lead_ref.shape[2]
    moves = [(src.at[pl.ds(0, RIM), pl.ds(0, lead)], lead_ref.at[at]) for at, src in enumerate((k_ref, v_ref))]
    moves += [(k_ref, k_out), (v_ref, v_out), (q_ref, q_out), (g_ref, g_out)]
    copies = [pltpu.make_async_copy(src, dst, sems.at[at]) for at, (src, dst) in enumerate(moves)]
    for copy in copies:
        copy.start()
    for copy in copies:
        copy.wait()


def own_kernel(
    count_ref, live_ref, lists_ref, q_ref, k_ref, v_ref, g_ref, table_ref, stats_ref, lead_b_ref, lead_i_ref
):
    tok = q_ref.shape[0]
    blocks = lists_ref.shape[0]
    count = count_ref[0]
    row = lax.broadcasted_iota(jnp.int32, (blocks, 1), 0)
    live = jnp.zeros_like(row)
    for n in range(blocks):
        live = jnp.where(row == n, live_ref[n], live)
    odd = lax.axis_index("band") % 2
    slot = lax.broadcasted_iota(jnp.int32, (blocks, TABLE), 1)
    x_first = 8 + RB * odd
    i_first = 8 + RB * (1 - odd)
    ids = jnp.where(slot < 8, slot, jnp.where(slot < 8 + RB, slot - 8 + x_first, slot - 8 - RB + i_first))
    ids = jnp.where(slot < 8 + 2 * RB, ids, -1)
    table = table_of(lists_ref[...], live, ids, count, tok)
    table_ref[:TABLE] = table
    past = lax.broadcasted_iota(jnp.int32, (tok - RIM, tok), 0) + RIM >= count
    tail = [jnp.broadcast_to(table[at : at + 1], (BLK, tok)) for at in range(RB, tok // BLK)]
    table_ref[TABLE:] = jnp.where(past, NEG, jnp.concatenate(tail, axis=0))
    for h in range(HEADS):
        q, k, v, g = (ref[:, cols(h)] for ref in (q_ref, k_ref, v_ref, g_ref))
        for at, lead in enumerate((k, v)):
            lead_i_ref[at, :, cols(h)] = lead[:RIM]
            if h >= SPLIT:
                lead_b_ref[at, :, cols(h - SPLIT)] = lead[:RIM]
        x = own_score(k, q, table_ref)
        top, total, raw = stats_of(x, nt(v, g))
        stats_ref[h] = jnp.concatenate([top, total, raw, jnp.zeros((5, tok), jnp.float32)], axis=0)


def rim_kernel(first, q_ref, g_ref, x_ref, i_ref, table_ref, stats_ref, *refs):
    gx_ref, gi_ref, final_ref, dq_ref = refs[-4:]
    if GATHER:
        i_ref = i_ref.at[1 - lax.axis_index("band") % 2]
    tok = q_ref.shape[0]
    if first:
        gi_ref[0] = refs[0][...]
        gi_ref = gi_ref.at[1]
    for at in range(x_ref.shape[2] // DEPTH):
        h = first + at
        q, g = q_ref[:, cols(h)], g_ref[:, cols(h)]
        score_x = biased(nt(x_ref[0, :, cols(at)], q), table_ref, 8)
        prod_x = nt(x_ref[1, :, cols(at)], g)
        score_i = biased(nt(i_ref[0, :, cols(h)], q), table_ref, 8 + RB)
        prod_i = nt(i_ref[1, :, cols(h)], g)
        own = (stats_ref[h, 0:1], stats_ref[h, 1:2], stats_ref[h, 2:3])
        top, total, raw = merged(own, merged(stats_of(score_x, prod_x), stats_of(score_i, prod_i)))
        inv = jnp.where(total > 0.0, 1.0 / jnp.where(total > 0.0, total, 1.0), 0.0)
        delta = raw * inv
        w, ds = grads_of(score_x, prod_x, top, inv, delta)
        gx_ref[0, :, cols(at)] = nn(ds, q).astype(jnp.bfloat16)
        gx_ref[1, :, cols(at)] = nn(w, g).astype(jnp.bfloat16)
        dq = tn(x_ref[0, :, cols(at)], ds)
        w, ds = grads_of(score_i, prod_i, top, inv, delta)
        gi_ref[0, :, cols(at)] = nn(ds, q).astype(jnp.bfloat16)
        gi_ref[1, :, cols(at)] = nn(w, g).astype(jnp.bfloat16)
        dq_ref[at] = dq + tn(i_ref[0, :, cols(h)], ds)
        final_ref[at] = jnp.concatenate([top, inv, delta, jnp.zeros((5, tok), jnp.float32)], axis=0)


def rest_of(first, at, q_ref, k_ref, v_ref, g_ref, table_ref, final_ref, rim_dq_ref):
    h = first + at
    q, k, v, g = (ref[:, cols(h)] for ref in (q_ref, k_ref, v_ref, g_ref))
    top, inv, delta = final_ref[at, 0:1], final_ref[at, 1:2], final_ref[at, 2:3]
    x = own_score(k, q, table_ref)
    w, ds = grads_of(x, nt(v, g), top, inv, delta)
    dq = rim_dq_ref[at] + tn(k, ds)
    return dq.T.astype(jnp.bfloat16), nn(ds, q), nn(w, g)


def held_kernel(first, *refs):
    _, dq_ref, pk_ref, pv_ref, dq_buf, sems = refs[7:]
    copies = []
    for at in range(pk_ref.shape[1] // DEPTH):
        dq, pk_ref[:, cols(at)], pv_ref[:, cols(at)] = rest_of(first, at, *refs[:7])
        dq_buf[:, cols(at)] = dq
        copies.append(pltpu.make_async_copy(dq_buf.at[:, cols(at)], dq_ref.at[:, cols(first + at)], sems.at[at]))
        copies[-1].start()
    for copy in copies:
        copy.wait()


def done_kernel(first, *refs):
    gx_ref, gi_ref, _, dq_ref, dk_ref, dv_ref, dq_buf, dk_buf, dv_buf, sems = refs[7:]
    if GATHER:
        gi_ref = gi_ref.at[1 - lax.axis_index("band") % 2]
    copies = []
    for at in range(dq_buf.shape[1] // DEPTH):
        dq, dk, dv = rest_of(first, at, *refs[:7])
        dq_buf[:, cols(at)] = dq
        for slot, buf, part in ((0, dk_buf, dk), (1, dv_buf, dv)):
            lead = gx_ref[slot, :, cols(at)].astype(jnp.float32) + gi_ref[0, slot, :, cols(at)].astype(jnp.float32)
            buf[:RIM, cols(at)] = (part[:RIM] + lead).astype(jnp.bfloat16)
            buf[RIM:, cols(at)] = part[RIM:].astype(jnp.bfloat16)
        for n, (buf, out) in enumerate(((dq_buf, dq_ref), (dk_buf, dk_ref), (dv_buf, dv_ref))):
            copies.append(pltpu.make_async_copy(buf.at[:, cols(at)], out.at[:, cols(first + at)], sems.at[n, at]))
            copies[-1].start()
    for copy in copies:
        copy.wait()


def add_kernel(first, pk_ref, pv_ref, gx_ref, gi_ref, _k, _v, dk_ref, dv_ref, dk_buf, dv_buf, sems):
    width = pk_ref.shape[1]
    if GATHER:
        gi_ref = gi_ref.at[1 - lax.axis_index("band") % 2]
    copies = []
    for slot, (own, buf, out) in enumerate(((pk_ref, dk_buf, dk_ref), (pv_ref, dv_buf, dv_ref))):
        lead = gx_ref[slot].astype(jnp.float32) + gi_ref[1, slot].astype(jnp.float32)
        buf[:RIM] = (own[:RIM] + lead).astype(jnp.bfloat16)
        buf[RIM:] = own[RIM:].astype(jnp.bfloat16)
        copies.append(pltpu.make_async_copy(buf, out.at[:, pl.ds(first * DEPTH, width)], sems.at[slot]))
        copies[-1].start()
    for copy in copies:
        copy.wait()


VMEM = pl.BlockSpec(memory_space=pltpu.VMEM)
SMEM = pl.BlockSpec(memory_space=pltpu.SMEM)
HBM = pl.BlockSpec(memory_space=pltpu.HBM)
ANY = pl.BlockSpec(memory_space=pl.ANY)


def call(body, name, ins, outs, out_specs, args, scratch=(), alias=None, limit=24):
    return pl.pallas_call(
        body,
        in_specs=ins,
        out_specs=out_specs,
        out_shape=outs,
        scratch_shapes=scratch,
        input_output_aliases=alias or {},
        compiler_params=pltpu.CompilerParams(vmem_limit_bytes=int(limit * MIB)),
        cost_estimate=pl.CostEstimate(flops=1000, bytes_accessed=1000, transcendentals=0),
        name=name,
    )(*args)


def shape(*dims, dtype=jnp.bfloat16):
    return jax.ShapeDtypeStruct(dims, dtype)


def on_device(queries, keys, values, out_grad, band_counts, block_lists, slot_counts):
    tok, width = queries.shape
    f32 = functools.partial(shape, dtype=jnp.float32)
    cuts = ((0, SPLIT), (SPLIT, HEADS))
    part = HEADS - SPLIT
    lead_a, k, v, q, g = call(
        load_kernel,
        "load_bands",
        [HBM] * 4,
        [shape(2, RIM, SPLIT * DEPTH)] + [shape(tok, width)] * 4,
        [VMEM] * 5,
        (keys, values, queries, out_grad),
        [pltpu.SemaphoreType.DMA((6,))],
        limit=LOAD_LIMIT,
    )
    x_a = swap_across(lead_a)
    table, stats, lead_b, lead_i = call(
        own_kernel,
        "own_stats",
        [SMEM] * 2 + [VMEM] * 5,
        [f32(TABLE + tok - RIM, tok), f32(HEADS, 8, tok), shape(2, RIM, part * DEPTH), shape(2, RIM, width)],
        [VMEM] * 4,
        (band_counts, slot_counts, block_lists, q, k, v, g),
    )
    x_b = swap_across(lead_b)
    i = swap_inside(lead_i)

    def rim(first, x, *more):
        heads = x.shape[2] // DEPTH
        gi = (2, 2, RIM, x.shape[2]) if more else x.shape
        return call(
            functools.partial(rim_kernel, first),
            "rim_grads",
            [VMEM] * (6 + len(more)),
            [shape(*x.shape), shape(*gi), f32(heads, 8, tok), f32(heads, DEPTH, tok)],
            [VMEM] * 4,
            (q, g, x, i, table, stats) + more,
        )

    gx_a, gi_a, final_a, dq_a = rim(0, x_a)
    gx_a = swap_across(gx_a)
    gx_b, gi, final_b, dq_b = rim(SPLIT, x_b, gi_a)
    gx_b = swap_across(gx_b)
    gi = swap_inside(gi)

    dq, pk, pv = call(
        functools.partial(held_kernel, SPLIT),
        "held_grads",
        [VMEM] * 7 + [ANY],
        [shape(tok, width), f32(tok, part * DEPTH), f32(tok, part * DEPTH)],
        [ANY, VMEM, VMEM],
        (q, k, v, g, table, final_b, dq_b, gx_a),
        [pltpu.VMEM((tok, part * DEPTH), jnp.bfloat16), pltpu.SemaphoreType.DMA((part,))],
    )
    dq, dk, dv = call(
        functools.partial(done_kernel, 0),
        "done_grads",
        [VMEM] * 9 + [ANY],
        [shape(tok, width)] * 3,
        [ANY] * 3,
        (q, k, v, g, table, final_a, dq_a, gx_a, gi, dq),
        [pltpu.VMEM((tok, SPLIT * DEPTH), jnp.bfloat16)] * 3 + [pltpu.SemaphoreType.DMA((3, SPLIT))],
        {9: 0},
    )
    dk, dv = call(
        functools.partial(add_kernel, SPLIT),
        "add_rims",
        [VMEM] * 4 + [ANY] * 2,
        [shape(tok, width)] * 2,
        [ANY] * 2,
        (pk, pv, gx_b, gi, dk, dv),
        [pltpu.VMEM((tok, part * DEPTH), jnp.bfloat16)] * 2 + [pltpu.SemaphoreType.DMA((2,))],
        {4: 0, 5: 1},
    )
    return dq, dk, dv


def solution(mesh):
    placed = P(("member", "band"), None)
    flat = P(("member", "band"))
    return jax.shard_map(
        on_device,
        mesh=mesh,
        in_specs=(placed, placed, placed, placed, flat, placed, flat),
        out_specs=(placed, placed, placed),
        check_vma=False,
    )
```

```python
import functools
import jax
import jax.numpy as jnp
from jax import lax
from jax.experimental import pallas as pl
from jax.experimental.pallas import tpu as pltpu
from jax.sharding import PartitionSpec as P

HEADS = 8
DEPTH = 128
BLK = 32
RB = 6
RIM = RB * BLK
TABLE = 32
LOG2E = 1.4426950408889634
NEG = -1e30
FLOOR = -1e20
MIB = 1024 * 1024
LOAD_LIMIT = 51.1
SPLIT = 4
MEGA = 10**6
WEIGHT = {
    "load_bands": 1,
    "pack_leads": 1,
    "first_stats": 11000,
    "rim_grads": 1,
    "held_grads": 11000,
    "done_grads": 11000,
    "add_rims": 1,
}


def nt(a, b):
    return lax.dot_general(a, b, (((1,), (1,)), ((), ())), preferred_element_type=jnp.float32)


def tn(a, b):
    return lax.dot_general(a, b, (((0,), (0,)), ((), ())), preferred_element_type=jnp.float32)


def nn(a, b):
    return jnp.dot(a, b, preferred_element_type=jnp.float32)


def cols(h):
    return slice(h * DEPTH, (h + 1) * DEPTH)


def biased(score, bias, first):
    scaled = score * (DEPTH ** -0.5 * LOG2E)
    parts = [
        scaled[at * BLK : (at + 1) * BLK] + bias[first + at : first + at + 1, :]
        for at in range(score.shape[0] // BLK)
    ]
    return jnp.concatenate(parts, axis=0)


def table_of(lists, live, ids, count, tok):
    blocks, slots = lists.shape
    hit = jnp.zeros((blocks, ids.shape[1]), jnp.float32)
    for l in range(slots):
        hit = jnp.where((lists[:, l : l + 1] == ids) & (live > l), 1.0, hit)
    lane = lax.broadcasted_iota(jnp.int32, (blocks, tok), 1)
    row = lax.broadcasted_iota(jnp.int32, (blocks, tok), 0)
    spread = jnp.where((lane // BLK == row) & (lane < count), 1.0, 0.0)
    return jnp.where(tn(hit, spread) > 0.5, 0.0, NEG)


def own_score(k, q, bias):
    x = nt(k, q) * (DEPTH ** -0.5 * LOG2E)
    parts = [x[at * BLK : (at + 1) * BLK] + bias[at : at + 1, :] for at in range(RB)]
    return jnp.concatenate(parts + [x[RIM:] + bias[TABLE:, :]], axis=0)


def stats_of(x, prod):
    top = jnp.maximum(jnp.max(x, axis=0, keepdims=True), FLOOR)
    p = jnp.exp2(x - top)
    return top, jnp.sum(p, axis=0, keepdims=True), jnp.sum(p * prod, axis=0, keepdims=True)


def merged(a, b):
    top = jnp.maximum(a[0], b[0])
    fa, fb = jnp.exp2(a[0] - top), jnp.exp2(b[0] - top)
    return top, a[1] * fa + b[1] * fb, a[2] * fa + b[2] * fb


def grads_of(x, prod, top, inv, delta):
    p = jnp.exp2(x - top)
    w = (p * inv).astype(jnp.bfloat16)
    ds = (p * (inv * (DEPTH ** -0.5)) * (prod - delta)).astype(jnp.bfloat16)
    return w, ds


def swap_across(x):
    count = lax.axis_size("band")
    pairs = [(at, at + 1) for at in range(1, count - 1, 2)]
    return lax.ppermute(x, "band", pairs + [(b, a) for a, b in pairs])


def swap_inside(x):
    return lax.ppermute(x, "band", [(at, at ^ 1) for at in range(lax.axis_size("band"))])


def load_kernel(k_ref, v_ref, q_ref, g_ref, lead_a_ref, lead_b_ref, k_out, v_out, q_out, g_out, sems):
    moves = []
    for lead, first in ((lead_a_ref, 0), (lead_b_ref, k_ref.shape[1] - lead_b_ref.shape[2])):
        for at, src in enumerate((k_ref, v_ref)):
            moves.append((src.at[pl.ds(0, RIM), pl.ds(first, lead.shape[2])], lead.at[at]))
    moves += [(k_ref, k_out), (v_ref, v_out), (q_ref, q_out), (g_ref, g_out)]
    copies = [pltpu.make_async_copy(src, dst, sems.at[at]) for at, (src, dst) in enumerate(moves)]
    for copy in copies:
        copy.start()
    for copy in copies:
        copy.wait()


def pack_kernel(count_ref, live_ref, lists_ref, k_ref, v_ref, table_ref, lead_ref):
    tok = k_ref.shape[0]
    for at, ref in enumerate((k_ref, v_ref)):
        lead_ref[at] = ref[:RIM, :]
    blocks = lists_ref.shape[0]
    count = count_ref[...]
    row = lax.broadcasted_iota(jnp.int32, (blocks, blocks), 0)
    lane = lax.broadcasted_iota(jnp.int32, (blocks, blocks), 1)
    live = jnp.sum(jnp.where(row == lane, live_ref[...], 0), axis=1, keepdims=True)
    odd = lax.axis_index("band") % 2
    slot = lax.broadcasted_iota(jnp.int32, (blocks, TABLE), 1)
    x_first = 8 + RB * odd
    i_first = 8 + RB * (1 - odd)
    ids = jnp.where(slot < 8, slot, jnp.where(slot < 8 + RB, slot - 8 + x_first, slot - 8 - RB + i_first))
    ids = jnp.where(slot < 8 + 2 * RB, ids, -1)
    table = table_of(lists_ref[...], live, ids, count, tok)
    table_ref[:TABLE] = table
    past = lax.broadcasted_iota(jnp.int32, (tok - RIM, tok), 0) + RIM >= count
    tail = [jnp.broadcast_to(table[at : at + 1], (BLK, tok)) for at in range(RB, tok // BLK)]
    table_ref[TABLE:] = jnp.where(past, NEG, jnp.concatenate(tail, axis=0))


def first_kernel(q_ref, k_ref, v_ref, g_ref, x_ref, table_ref, stats_ref):
    tok = q_ref.shape[0]
    for h in range(stats_ref.shape[0]):
        q, k, v, g = (ref[:, cols(h)] for ref in (q_ref, k_ref, v_ref, g_ref))
        own = stats_of(own_score(k, q, table_ref), nt(v, g))
        rim = stats_of(biased(nt(x_ref[0, :, cols(h)], q), table_ref, 8), nt(x_ref[1, :, cols(h)], g))
        stats_ref[h] = jnp.concatenate(merged(own, rim) + (jnp.zeros((5, tok), jnp.float32),), axis=0)


def rim_kernel(first, q_ref, g_ref, x_ref, i_ref, table_ref, *refs):
    gx_ref, gi_ref, final_ref, dq_ref = refs[-4:]
    tok = q_ref.shape[0]
    if first:
        k_ref, v_ref, before = refs[:3]
        gi_ref[0] = before[...]
        gi_ref = gi_ref.at[1]
    else:
        stats_ref = refs[0]
    for at in range(x_ref.shape[2] // DEPTH):
        h = first + at
        q, g = q_ref[:, cols(h)], g_ref[:, cols(h)]
        score_x = biased(nt(x_ref[0, :, cols(at)], q), table_ref, 8)
        prod_x = nt(x_ref[1, :, cols(at)], g)
        score_i = biased(nt(i_ref[0, :, cols(h)], q), table_ref, 8 + RB)
        prod_i = nt(i_ref[1, :, cols(h)], g)
        if first:
            own = stats_of(own_score(k_ref[:, cols(h)], q, table_ref), nt(v_ref[:, cols(h)], g))
            known = merged(own, stats_of(score_x, prod_x))
        else:
            known = (stats_ref[h, 0:1], stats_ref[h, 1:2], stats_ref[h, 2:3])
        top, total, raw = merged(known, stats_of(score_i, prod_i))
        inv = jnp.where(total > 0.0, 1.0 / jnp.where(total > 0.0, total, 1.0), 0.0)
        delta = raw * inv
        w, ds = grads_of(score_x, prod_x, top, inv, delta)
        gx_ref[0, :, cols(at)] = nn(ds, q).astype(jnp.bfloat16)
        gx_ref[1, :, cols(at)] = nn(w, g).astype(jnp.bfloat16)
        dq = tn(x_ref[0, :, cols(at)], ds)
        w, ds = grads_of(score_i, prod_i, top, inv, delta)
        gi_ref[0, :, cols(at)] = nn(ds, q).astype(jnp.bfloat16)
        gi_ref[1, :, cols(at)] = nn(w, g).astype(jnp.bfloat16)
        dq_ref[at] = dq + tn(i_ref[0, :, cols(h)], ds)
        final_ref[at] = jnp.concatenate([top, inv, delta, jnp.zeros((5, tok), jnp.float32)], axis=0)


def rest_of(first, at, q_ref, k_ref, v_ref, g_ref, table_ref, final_ref, rim_dq_ref):
    h = first + at
    q, k, v, g = (ref[:, cols(h)] for ref in (q_ref, k_ref, v_ref, g_ref))
    top, inv, delta = final_ref[at, 0:1], final_ref[at, 1:2], final_ref[at, 2:3]
    x = own_score(k, q, table_ref)
    w, ds = grads_of(x, nt(v, g), top, inv, delta)
    dq = rim_dq_ref[at] + tn(k, ds)
    return dq.T.astype(jnp.bfloat16), nn(ds, q), nn(w, g)


def held_kernel(first, *refs):
    _, dq_ref, pk_ref, pv_ref, dq_buf, sems = refs[7:]
    copies = []
    for at in range(pk_ref.shape[1] // DEPTH):
        dq, pk_ref[:, cols(at)], pv_ref[:, cols(at)] = rest_of(first, at, *refs[:7])
        dq_buf[:, cols(at)] = dq
        copies.append(pltpu.make_async_copy(dq_buf.at[:, cols(at)], dq_ref.at[:, cols(first + at)], sems.at[at]))
        copies[-1].start()
    for copy in copies:
        copy.wait()


def done_kernel(first, *refs):
    gx_ref, gi_ref, _, dq_ref, dk_ref, dv_ref, dq_buf, dk_buf, dv_buf, sems = refs[7:]
    copies = []
    for at in range(dq_buf.shape[1] // DEPTH):
        dq, dk, dv = rest_of(first, at, *refs[:7])
        dq_buf[:, cols(at)] = dq
        for slot, buf, part in ((0, dk_buf, dk), (1, dv_buf, dv)):
            lead = gx_ref[slot, :, cols(at)].astype(jnp.float32) + gi_ref[0, slot, :, cols(at)].astype(jnp.float32)
            buf[:RIM, cols(at)] = (part[:RIM] + lead).astype(jnp.bfloat16)
            buf[RIM:, cols(at)] = part[RIM:].astype(jnp.bfloat16)
        for n, (buf, out) in enumerate(((dq_buf, dq_ref), (dk_buf, dk_ref), (dv_buf, dv_ref))):
            copies.append(pltpu.make_async_copy(buf.at[:, cols(at)], out.at[:, cols(first + at)], sems.at[n, at]))
            copies[-1].start()
    for copy in copies:
        copy.wait()


def add_kernel(first, pk_ref, pv_ref, gx_ref, gi_ref, _k, _v, dk_ref, dv_ref, dk_buf, dv_buf, sems):
    width = pk_ref.shape[1]
    copies = []
    for slot, (own, buf, out) in enumerate(((pk_ref, dk_buf, dk_ref), (pv_ref, dv_buf, dv_ref))):
        lead = gx_ref[slot].astype(jnp.float32) + gi_ref[1, slot].astype(jnp.float32)
        buf[:RIM] = (own[:RIM] + lead).astype(jnp.bfloat16)
        buf[RIM:] = own[RIM:].astype(jnp.bfloat16)
        copies.append(pltpu.make_async_copy(buf, out.at[:, pl.ds(first * DEPTH, width)], sems.at[slot]))
        copies[-1].start()
    for copy in copies:
        copy.wait()


VMEM = pl.BlockSpec(memory_space=pltpu.VMEM)
HBM = pl.BlockSpec(memory_space=pltpu.HBM)
ANY = pl.BlockSpec(memory_space=pl.ANY)


def call(body, name, ins, outs, out_specs, args, scratch=(), alias=None, limit=24):
    return pl.pallas_call(
        body,
        in_specs=ins,
        out_specs=out_specs,
        out_shape=outs,
        scratch_shapes=scratch,
        input_output_aliases=alias or {},
        compiler_params=pltpu.CompilerParams(vmem_limit_bytes=int(limit * MIB)),
        cost_estimate=pl.CostEstimate(flops=WEIGHT[name] * MEGA, bytes_accessed=1000, transcendentals=0),
        name=name,
    )(*args)


def shape(*dims, dtype=jnp.bfloat16):
    return jax.ShapeDtypeStruct(dims, dtype)


def on_device(queries, keys, values, out_grad, band_counts, block_lists, slot_counts):
    tok, width = queries.shape
    f32 = functools.partial(shape, dtype=jnp.float32)
    cuts = ((0, SPLIT), (SPLIT, HEADS))
    part = HEADS - SPLIT
    lead_a, lead_b, k, v, q, g = call(
        load_kernel,
        "load_bands",
        [HBM] * 4,
        [shape(2, RIM, SPLIT * DEPTH), shape(2, RIM, part * DEPTH)] + [shape(tok, width)] * 4,
        [VMEM] * 6,
        (keys, values, queries, out_grad),
        [pltpu.SemaphoreType.DMA((8,))],
        limit=LOAD_LIMIT,
    )
    x_a, x_b = swap_across(lead_a), swap_across(lead_b)
    table, lead_i = call(
        pack_kernel,
        "pack_leads",
        [VMEM] * 5,
        [f32(TABLE + tok - RIM, tok), shape(2, RIM, width)],
        [VMEM] * 2,
        (band_counts[:, None], slot_counts[None], block_lists, k, v),
    )
    i = swap_inside(lead_i)
    stats_a = call(
        first_kernel, "first_stats", [VMEM] * 6, f32(SPLIT, 8, tok), VMEM, (q, k, v, g, x_a, table)
    )

    def rim(first, x, *more):
        heads = x.shape[2] // DEPTH
        gi = (2, 2, RIM, x.shape[2]) if first else x.shape
        return call(
            functools.partial(rim_kernel, first),
            "rim_grads",
            [VMEM] * (5 + len(more)),
            [shape(*x.shape), shape(*gi), f32(heads, 8, tok), f32(heads, DEPTH, tok)],
            [VMEM] * 4,
            (q, g, x, i, table) + more,
        )

    gx_a, gi_a, final_a, dq_a = rim(0, x_a, stats_a)
    gx_a = swap_across(gx_a)
    gx_b, gi, final_b, dq_b = rim(SPLIT, x_b, k, v, gi_a)
    gx_b = swap_across(gx_b)
    gi = swap_inside(gi)

    dq, pk, pv = call(
        functools.partial(held_kernel, SPLIT),
        "held_grads",
        [VMEM] * 7 + [ANY],
        [shape(tok, width), f32(tok, part * DEPTH), f32(tok, part * DEPTH)],
        [ANY, VMEM, VMEM],
        (q, k, v, g, table, final_b, dq_b, gx_a),
        [pltpu.VMEM((tok, part * DEPTH), jnp.bfloat16), pltpu.SemaphoreType.DMA((part,))],
    )
    dq, dk, dv = call(
        functools.partial(done_kernel, 0),
        "done_grads",
        [VMEM] * 9 + [ANY],
        [shape(tok, width)] * 3,
        [ANY] * 3,
        (q, k, v, g, table, final_a, dq_a, gx_a, gi, dq),
        [pltpu.VMEM((tok, SPLIT * DEPTH), jnp.bfloat16)] * 3 + [pltpu.SemaphoreType.DMA((3, SPLIT))],
        {9: 0},
    )
    dk, dv = call(
        functools.partial(add_kernel, SPLIT),
        "add_rims",
        [VMEM] * 4 + [ANY] * 2,
        [shape(tok, width)] * 2,
        [ANY] * 2,
        (pk, pv, gx_b, gi, dk, dv),
        [pltpu.VMEM((tok, part * DEPTH), jnp.bfloat16)] * 2 + [pltpu.SemaphoreType.DMA((2,))],
        {4: 0, 5: 1},
    )
    return dq, dk, dv


def solution(mesh):
    placed = P(("member", "band"), None)
    flat = P(("member", "band"))
    return jax.shard_map(
        on_device,
        mesh=mesh,
        in_specs=(placed, placed, placed, placed, flat, placed, flat),
        out_specs=(placed, placed, placed),
        check_vma=False,
    )
```

```python
import functools
import jax
import jax.numpy as jnp
from jax import lax
from jax.experimental import pallas as pl
from jax.experimental.pallas import tpu as pltpu
from jax.sharding import PartitionSpec as P

HEADS = 8
DEPTH = 128
BLK = 32
RB = 6
RIM = RB * BLK
TABLE = 32
LOG2E = 1.4426950408889634
NEG = -1e30
FLOOR = -1e20
MIB = 1024 * 1024
LOAD_LIMIT = 53.14
SPLIT = 4
MEGA = 10**6
WEIGHT = {
    "load_bands": 5500,
    "pack_leads": 1,
    "own_stats": 1,
    "first_stats": 11000,
    "rim_grads": 1,
    "inside_grads": 1,
    "held_grads": 11000,
    "done_grads": 11000,
    "add_rims": 1,
}


def nt(a, b):
    return lax.dot_general(a, b, (((1,), (1,)), ((), ())), preferred_element_type=jnp.float32)


def tn(a, b):
    return lax.dot_general(a, b, (((0,), (0,)), ((), ())), preferred_element_type=jnp.float32)


def nn(a, b):
    return jnp.dot(a, b, preferred_element_type=jnp.float32)


def cols(h):
    return slice(h * DEPTH, (h + 1) * DEPTH)


def biased(score, bias, first):
    scaled = score * (DEPTH ** -0.5 * LOG2E)
    parts = [
        scaled[at * BLK : (at + 1) * BLK] + bias[first + at : first + at + 1, :]
        for at in range(score.shape[0] // BLK)
    ]
    return jnp.concatenate(parts, axis=0)


def table_of(lists, live, ids, count, tok):
    blocks, slots = lists.shape
    hit = jnp.zeros((blocks, ids.shape[1]), jnp.float32)
    for l in range(slots):
        hit = jnp.where((lists[:, l : l + 1] == ids) & (live > l), 1.0, hit)
    lane = lax.broadcasted_iota(jnp.int32, (blocks, tok), 1)
    row = lax.broadcasted_iota(jnp.int32, (blocks, tok), 0)
    spread = jnp.where((lane // BLK == row) & (lane < count), 1.0, 0.0)
    return jnp.where(tn(hit, spread) > 0.5, 0.0, NEG)


def own_score(k, q, bias):
    x = nt(k, q) * (DEPTH ** -0.5 * LOG2E)
    parts = [x[at * BLK : (at + 1) * BLK] + bias[at : at + 1, :] for at in range(RB)]
    return jnp.concatenate(parts + [x[RIM:] + bias[TABLE:, :]], axis=0)


def merged(a, b):
    top = jnp.maximum(a[0], b[0])
    fa, fb = jnp.exp2(a[0] - top), jnp.exp2(b[0] - top)
    return top, a[1] * fa + b[1] * fb, a[2] * fa + b[2] * fb


def held_of(x, prod, p_ref, prod_ref):
    top = jnp.maximum(jnp.max(x, axis=0, keepdims=True), FLOOR)
    p = jnp.exp2(x - top)
    p_ref[...] = p
    prod_ref[...] = prod
    return top, jnp.sum(p, axis=0, keepdims=True), jnp.sum(p * prod, axis=0, keepdims=True)


def rows_of(values):
    pad = jnp.zeros((8 - len(values), values[0].shape[1]), jnp.float32)
    return jnp.concatenate(tuple(values) + (pad,), axis=0)


def known(ref):
    return ref[0:1], ref[1:2], ref[2:3]


def grads_of(p, prod, factor, delta):
    w = (p * factor).astype(jnp.bfloat16)
    ds = (p * (factor * (DEPTH ** -0.5)) * (prod - delta)).astype(jnp.bfloat16)
    return w, ds


def swap_across(x):
    count = lax.axis_size("band")
    pairs = [(at, at + 1) for at in range(1, count - 1, 2)]
    return lax.ppermute(x, "band", pairs + [(b, a) for a, b in pairs])


def swap_inside(x):
    return lax.ppermute(x, "band", [(at, at ^ 1) for at in range(lax.axis_size("band"))])


def load_kernel(k_ref, v_ref, lead_a_ref, lead_b_ref, sems):
    moves = []
    for lead, first in ((lead_a_ref, 0), (lead_b_ref, k_ref.shape[1] - lead_b_ref.shape[2])):
        for at, src in enumerate((k_ref, v_ref)):
            moves.append((src.at[pl.ds(0, RIM), pl.ds(first, lead.shape[2])], lead.at[at]))
    copies = [pltpu.make_async_copy(src, dst, sems.at[at]) for at, (src, dst) in enumerate(moves)]
    for copy in copies:
        copy.start()
    for copy in copies:
        copy.wait()


def pack_kernel(k_ref, v_ref, lead_ref):
    for at, ref in enumerate((k_ref, v_ref)):
        lead_ref[at] = ref[:RIM, :]


def own_kernel(count_ref, live_ref, lists_ref, q_ref, k_ref, v_ref, g_ref, table_ref, stats_ref, p_ref, prod_ref):
    tok = q_ref.shape[0]
    blocks = lists_ref.shape[0]
    count = count_ref[...]
    row = lax.broadcasted_iota(jnp.int32, (blocks, blocks), 0)
    lane = lax.broadcasted_iota(jnp.int32, (blocks, blocks), 1)
    live = jnp.sum(jnp.where(row == lane, live_ref[...], 0), axis=1, keepdims=True)
    odd = lax.axis_index("band") % 2
    slot = lax.broadcasted_iota(jnp.int32, (blocks, TABLE), 1)
    x_first = 8 + RB * odd
    i_first = 8 + RB * (1 - odd)
    ids = jnp.where(slot < 8, slot, jnp.where(slot < 8 + RB, slot - 8 + x_first, slot - 8 - RB + i_first))
    ids = jnp.where(slot < 8 + 2 * RB, ids, -1)
    table = table_of(lists_ref[...], live, ids, count, tok)
    table_ref[:TABLE] = table
    past = lax.broadcasted_iota(jnp.int32, (tok - RIM, tok), 0) + RIM >= count
    tail = [jnp.broadcast_to(table[at : at + 1], (BLK, tok)) for at in range(RB, tok // BLK)]
    table_ref[TABLE:] = jnp.where(past, NEG, jnp.concatenate(tail, axis=0))
    for h in range(HEADS):
        q, k, v, g = (ref[:, cols(h)] for ref in (q_ref, k_ref, v_ref, g_ref))
        stats_ref[h] = rows_of(held_of(own_score(k, q, table_ref), nt(v, g), p_ref.at[h], prod_ref.at[h]))


def first_kernel(q_ref, g_ref, x_ref, table_ref, stats_ref, p_ref, prod_ref):
    for h in range(SPLIT):
        q, g = q_ref[:, cols(h)], g_ref[:, cols(h)]
        x = biased(nt(x_ref[0, :, cols(h)], q), table_ref, 8)
        stats_ref[h] = rows_of(held_of(x, nt(x_ref[1, :, cols(h)], g), p_ref.at[h], prod_ref.at[h]))


def rim_kernel(first, q_ref, g_ref, x_ref, i_ref, table_ref, stats_ref, *refs):
    gx_ref, final_ref, dq_ref, pi_ref, prodi_ref = refs[-5:]
    for at in range(x_ref.shape[2] // DEPTH):
        h = first + at
        q, g = q_ref[:, cols(h)], g_ref[:, cols(h)]
        x = biased(nt(i_ref[0, :, cols(h)], q), table_ref, 8 + RB)
        part_i = held_of(x, nt(i_ref[1, :, cols(h)], g), pi_ref.at[at], prodi_ref.at[at])
        if first:
            score, prod = biased(nt(x_ref[0, :, cols(at)], q), table_ref, 8), nt(x_ref[1, :, cols(at)], g)
            top = jnp.maximum(jnp.max(score, axis=0, keepdims=True), FLOOR)
            p = jnp.exp2(score - top)
            part_x = top, jnp.sum(p, axis=0, keepdims=True), jnp.sum(p * prod, axis=0, keepdims=True)
        else:
            stats_x_ref, px_ref, prodx_ref = refs[:3]
            part_x, p, prod = known(stats_x_ref.at[h]), px_ref[h], prodx_ref[h]
        own = known(stats_ref.at[h])
        top, total, raw = merged(merged(own, part_i), part_x)
        inv = jnp.where(total > 0.0, 1.0 / jnp.where(total > 0.0, total, 1.0), 0.0)
        delta = raw * inv
        w, ds = grads_of(p, prod, jnp.exp2(part_x[0] - top) * inv, delta)
        gx_ref[0, :, cols(at)] = nn(ds, q).astype(jnp.bfloat16)
        gx_ref[1, :, cols(at)] = nn(w, g).astype(jnp.bfloat16)
        dq_ref[at] = tn(x_ref[0, :, cols(at)], ds)
        final_ref[at] = rows_of((jnp.exp2(own[0] - top) * inv, jnp.exp2(part_i[0] - top) * inv, delta))


def inside_kernel(q_ref, g_ref, i_ref, *refs):
    gi_ref, dq_ref = refs[-2:]
    for h in range(HEADS):
        final_ref, rim_dq_ref, pi_ref, prodi_ref = refs[:4] if h < SPLIT else refs[4:8]
        at = h if h < SPLIT else h - SPLIT
        q, g = q_ref[:, cols(h)], g_ref[:, cols(h)]
        w, ds = grads_of(pi_ref[at], prodi_ref[at], final_ref[at, 1:2], final_ref[at, 2:3])
        gi_ref[0, :, cols(h)] = nn(ds, q).astype(jnp.bfloat16)
        gi_ref[1, :, cols(h)] = nn(w, g).astype(jnp.bfloat16)
        dq_ref[h] = rim_dq_ref[at] + tn(i_ref[0, :, cols(h)], ds)


def rest_of(first, at, q_ref, k_ref, g_ref, p_ref, prod_ref, final_ref, rim_dq_ref):
    h = first + at
    q, k, g = (ref[:, cols(h)] for ref in (q_ref, k_ref, g_ref))
    w, ds = grads_of(p_ref[h], prod_ref[h], final_ref[at, 0:1], final_ref[at, 2:3])
    dq = rim_dq_ref[h] + tn(k, ds)
    return dq.T.astype(jnp.bfloat16), nn(ds, q), nn(w, g)


def held_kernel(first, *refs):
    _, dq_ref, pk_ref, pv_ref, dq_buf, sems = refs[7:]
    copies = []
    for at in range(pk_ref.shape[1] // DEPTH):
        dq, pk_ref[:, cols(at)], pv_ref[:, cols(at)] = rest_of(first, at, *refs[:7])
        dq_buf[:, cols(at)] = dq
        copies.append(pltpu.make_async_copy(dq_buf.at[:, cols(at)], dq_ref.at[:, cols(first + at)], sems.at[at]))
        copies[-1].start()
    for copy in copies:
        copy.wait()


def done_kernel(first, *refs):
    gx_ref, gi_ref, _, dq_ref, dk_ref, dv_ref, dq_buf, dk_buf, dv_buf, sems = refs[7:]
    copies = []
    for at in range(dq_buf.shape[1] // DEPTH):
        dq, dk, dv = rest_of(first, at, *refs[:7])
        dq_buf[:, cols(at)] = dq
        for slot, buf, part in ((0, dk_buf, dk), (1, dv_buf, dv)):
            lead = gx_ref[slot, :, cols(at)].astype(jnp.float32) + gi_ref[slot, :, cols(first + at)].astype(jnp.float32)
            buf[:RIM, cols(at)] = (part[:RIM] + lead).astype(jnp.bfloat16)
            buf[RIM:, cols(at)] = part[RIM:].astype(jnp.bfloat16)
        for n, (buf, out) in enumerate(((dq_buf, dq_ref), (dk_buf, dk_ref), (dv_buf, dv_ref))):
            copies.append(pltpu.make_async_copy(buf.at[:, cols(at)], out.at[:, cols(first + at)], sems.at[n, at]))
            copies[-1].start()
    for copy in copies:
        copy.wait()


def add_kernel(first, pk_ref, pv_ref, gx_ref, gi_ref, _k, _v, dk_ref, dv_ref, dk_buf, dv_buf, sems):
    copies = []
    for at in range(pk_ref.shape[1] // DEPTH):
        for slot, (own, buf, out) in enumerate(((pk_ref, dk_buf, dk_ref), (pv_ref, dv_buf, dv_ref))):
            lead = gx_ref[slot, :, cols(at)].astype(jnp.float32) + gi_ref[slot, :, cols(first + at)].astype(jnp.float32)
            buf[:RIM, cols(at)] = (own[:RIM, cols(at)] + lead).astype(jnp.bfloat16)
            buf[RIM:, cols(at)] = own[RIM:, cols(at)].astype(jnp.bfloat16)
            copies.append(pltpu.make_async_copy(buf.at[:, cols(at)], out.at[:, cols(first + at)], sems.at[slot, at]))
            copies[-1].start()
    for copy in copies:
        copy.wait()


VMEM = pl.BlockSpec(memory_space=pltpu.VMEM)
HBM = pl.BlockSpec(memory_space=pltpu.HBM)
ANY = pl.BlockSpec(memory_space=pl.ANY)


def call(body, name, ins, outs, out_specs, args, scratch=(), alias=None, limit=24):
    return pl.pallas_call(
        body,
        in_specs=ins,
        out_specs=out_specs,
        out_shape=outs,
        scratch_shapes=scratch,
        input_output_aliases=alias or {},
        compiler_params=pltpu.CompilerParams(vmem_limit_bytes=int(limit * MIB)),
        cost_estimate=pl.CostEstimate(flops=WEIGHT[name] * MEGA, bytes_accessed=1000, transcendentals=0),
        name=name,
    )(*args)


def shape(*dims, dtype=jnp.bfloat16):
    return jax.ShapeDtypeStruct(dims, dtype)


def on_device(queries, keys, values, out_grad, band_counts, block_lists, slot_counts):
    tok, width = queries.shape
    f32 = functools.partial(shape, dtype=jnp.float32)
    cuts = ((0, SPLIT), (SPLIT, HEADS))
    part = HEADS - SPLIT
    q, k, v, g = queries, keys, values, out_grad
    lead_a, lead_b = call(
        load_kernel,
        "load_bands",
        [HBM] * 2,
        [shape(2, RIM, SPLIT * DEPTH), shape(2, RIM, part * DEPTH)],
        [VMEM] * 2,
        (keys, values),
        [pltpu.SemaphoreType.DMA((4,))],
        limit=LOAD_LIMIT,
    )
    x_a, x_b = swap_across(lead_a), swap_across(lead_b)
    lead_i = call(pack_kernel, "pack_leads", [VMEM] * 2, shape(2, RIM, width), VMEM, (k, v))
    i = swap_inside(lead_i)
    table, stats, p, prod = call(
        own_kernel,
        "own_stats",
        [VMEM] * 7,
        [f32(TABLE + tok - RIM, tok), f32(HEADS, 8, tok), f32(HEADS, tok, tok), f32(HEADS, tok, tok)],
        [VMEM] * 4,
        (band_counts[:, None], slot_counts[None], block_lists, q, k, v, g),
    )
    stats_x, px, prodx = call(
        first_kernel,
        "first_stats",
        [VMEM] * 4,
        [f32(SPLIT, 8, tok), f32(SPLIT, RIM, tok), f32(SPLIT, RIM, tok)],
        [VMEM] * 3,
        (q, g, x_a, table),
    )

    def rim(first, x, *more):
        heads = x.shape[2] // DEPTH
        return call(
            functools.partial(rim_kernel, first),
            "rim_grads",
            [VMEM] * (6 + len(more)),
            [shape(*x.shape), f32(heads, 8, tok), f32(heads, DEPTH, tok), f32(heads, RIM, tok), f32(heads, RIM, tok)],
            [VMEM] * 5,
            (q, g, x, i, table, stats) + more,
        )

    gx_a, *rest_a = rim(0, x_a, stats_x, px, prodx)
    gx_a = swap_across(gx_a)
    gx_b, *rest_b = rim(SPLIT, x_b)
    gx_b = swap_across(gx_b)
    gi, dq_rim = call(
        inside_kernel,
        "inside_grads",
        [VMEM] * 11,
        [shape(2, RIM, width), f32(HEADS, DEPTH, tok)],
        [VMEM] * 2,
        (q, g, i, *rest_a, *rest_b),
    )
    gi = swap_inside(gi)

    dq, pk, pv = call(
        functools.partial(held_kernel, SPLIT),
        "held_grads",
        [VMEM] * 7 + [ANY],
        [shape(tok, width), f32(tok, part * DEPTH), f32(tok, part * DEPTH)],
        [ANY, VMEM, VMEM],
        (q, k, g, p, prod, rest_b[0], dq_rim, gx_a),
        [pltpu.VMEM((tok, part * DEPTH), jnp.bfloat16), pltpu.SemaphoreType.DMA((part,))],
    )
    dq, dk, dv = call(
        functools.partial(done_kernel, 0),
        "done_grads",
        [VMEM] * 9 + [ANY],
        [shape(tok, width)] * 3,
        [ANY] * 3,
        (q, k, g, p, prod, rest_a[0], dq_rim, gx_a, gi, dq),
        [pltpu.VMEM((tok, SPLIT * DEPTH), jnp.bfloat16)] * 3 + [pltpu.SemaphoreType.DMA((3, SPLIT))],
        {9: 0},
    )
    dk, dv = call(
        functools.partial(add_kernel, SPLIT),
        "add_rims",
        [VMEM] * 4 + [ANY] * 2,
        [shape(tok, width)] * 2,
        [ANY] * 2,
        (pk, pv, gx_b, gi, dk, dv),
        [pltpu.VMEM((tok, part * DEPTH), jnp.bfloat16)] * 2 + [pltpu.SemaphoreType.DMA((2, part))],
        {4: 0, 5: 1},
    )
    return dq, dk, dv


def solution(mesh):
    placed = P(("member", "band"), None)
    flat = P(("member", "band"))
    return jax.shard_map(
        on_device,
        mesh=mesh,
        in_specs=(placed, placed, placed, placed, flat, placed, flat),
        out_specs=(placed, placed, placed),
        check_vma=False,
    )
```

```python
import functools
import jax
import jax.numpy as jnp
from jax import lax
from jax.experimental import pallas as pl
from jax.experimental.pallas import tpu as pltpu
from jax.sharding import PartitionSpec as P

HEADS = 8
DEPTH = 128
BLK = 32
RB = 6
RIM = RB * BLK
TABLE = 32
LOG2E = 1.4426950408889634
NEG = -1e30
FLOOR = -1e20
MIB = 1024 * 1024
LOAD_LIMIT = 53.14
SPLIT = 4
MEGA = 10**6
WEIGHT = {
    "load_bands": 5500,
    "pack_leads": 1,
    "own_stats": 1,
    "first_stats": 11000,
    "rim_grads": 1,
    "inside_grads": 1,
    "held_grads": 11000,
    "done_grads": 11000,
    "add_rims": 1,
}


def nt(a, b):
    return lax.dot_general(a, b, (((1,), (1,)), ((), ())), preferred_element_type=jnp.float32)


def tn(a, b):
    return lax.dot_general(a, b, (((0,), (0,)), ((), ())), preferred_element_type=jnp.float32)


def nn(a, b):
    return jnp.dot(a, b, preferred_element_type=jnp.float32)


def cols(h):
    return slice(h * DEPTH, (h + 1) * DEPTH)


SCALE = DEPTH ** -0.5 * LOG2E


def exps_of(score, bias, first):
    parts = [score[at * BLK : (at + 1) * BLK] for at in range(score.shape[0] // BLK)]
    rows = [bias[first + at : first + at + 1, :] for at in range(len(parts))]
    tops = [jnp.max(part, axis=0, keepdims=True) * SCALE + row for part, row in zip(parts, rows)]
    top = functools.reduce(jnp.maximum, tops, jnp.full_like(tops[0], FLOOR))
    return top, jnp.concatenate([jnp.exp2(part * SCALE + (row - top)) for part, row in zip(parts, rows)], axis=0)


def own_exps(score, bias):
    lead, tail = score[:RIM], score[RIM:] * SCALE + bias[TABLE:, :]
    parts = [lead[at * BLK : (at + 1) * BLK] for at in range(RB)]
    rows = [bias[at : at + 1, :] for at in range(RB)]
    tops = [jnp.max(part, axis=0, keepdims=True) * SCALE + row for part, row in zip(parts, rows)]
    top = functools.reduce(jnp.maximum, tops, jnp.maximum(jnp.max(tail, axis=0, keepdims=True), FLOOR))
    exps = [jnp.exp2(part * SCALE + (row - top)) for part, row in zip(parts, rows)]
    return top, jnp.concatenate(exps + [jnp.exp2(tail - top)], axis=0)


def table_of(lists, live, ids, count, tok):
    blocks, slots = lists.shape
    hit = jnp.zeros((blocks, ids.shape[1]), jnp.float32)
    for l in range(slots):
        hit = jnp.where((lists[:, l : l + 1] == ids) & (live > l), 1.0, hit)
    lane = lax.broadcasted_iota(jnp.int32, (blocks, tok), 1)
    row = lax.broadcasted_iota(jnp.int32, (blocks, tok), 0)
    spread = jnp.where((lane // BLK == row) & (lane < count), 1.0, 0.0)
    return jnp.where(tn(hit, spread) > 0.5, 0.0, NEG)


def merged(a, b):
    top = jnp.maximum(a[0], b[0])
    fa, fb = jnp.exp2(a[0] - top), jnp.exp2(b[0] - top)
    return top, a[1] * fa + b[1] * fb, a[2] * fa + b[2] * fb


def sums_of(top, p, prod):
    return top, jnp.sum(p, axis=0, keepdims=True), jnp.sum(p * prod, axis=0, keepdims=True)


def rows_of(values):
    pad = jnp.zeros((8 - len(values), values[0].shape[1]), jnp.float32)
    return jnp.concatenate(tuple(values) + (pad,), axis=0)


def known(ref):
    return ref[0:1], ref[1:2], ref[2:3]


def grads_of(p, prod, factor, delta):
    w = (p * factor).astype(jnp.bfloat16)
    ds = (p * (factor * (DEPTH ** -0.5)) * (prod - delta)).astype(jnp.bfloat16)
    return w, ds


def swap_across(x):
    count = lax.axis_size("band")
    pairs = [(at, at + 1) for at in range(1, count - 1, 2)]
    return lax.ppermute(x, "band", pairs + [(b, a) for a, b in pairs])


def swap_inside(x):
    return lax.ppermute(x, "band", [(at, at ^ 1) for at in range(lax.axis_size("band"))])


def load_kernel(k_ref, v_ref, lead_a_ref, lead_b_ref, sems):
    moves = []
    for lead, first in ((lead_a_ref, 0), (lead_b_ref, k_ref.shape[1] - lead_b_ref.shape[2])):
        for at, src in enumerate((k_ref, v_ref)):
            moves.append((src.at[pl.ds(0, RIM), pl.ds(first, lead.shape[2])], lead.at[at]))
    copies = [pltpu.make_async_copy(src, dst, sems.at[at]) for at, (src, dst) in enumerate(moves)]
    for copy in copies:
        copy.start()
    for copy in copies:
        copy.wait()


def pack_kernel(k_ref, v_ref, lead_ref):
    for at, ref in enumerate((k_ref, v_ref)):
        lead_ref[at] = ref[:RIM, :]


def own_kernel(count_ref, live_ref, lists_ref, q_ref, k_ref, v_ref, g_ref, table_ref, stats_ref, p_ref, prod_ref):
    tok = q_ref.shape[0]
    blocks = lists_ref.shape[0]
    count = count_ref[...]
    row = lax.broadcasted_iota(jnp.int32, (blocks, blocks), 0)
    lane = lax.broadcasted_iota(jnp.int32, (blocks, blocks), 1)
    live = jnp.sum(jnp.where(row == lane, live_ref[...], 0), axis=1, keepdims=True)
    odd = lax.axis_index("band") % 2
    slot = lax.broadcasted_iota(jnp.int32, (blocks, TABLE), 1)
    x_first = 8 + RB * odd
    i_first = 8 + RB * (1 - odd)
    ids = jnp.where(slot < 8, slot, jnp.where(slot < 8 + RB, slot - 8 + x_first, slot - 8 - RB + i_first))
    ids = jnp.where(slot < 8 + 2 * RB, ids, -1)
    table = table_of(lists_ref[...], live, ids, count, tok)
    table_ref[:TABLE] = table
    past = lax.broadcasted_iota(jnp.int32, (tok - RIM, tok), 0) + RIM >= count
    tail = [jnp.broadcast_to(table[at : at + 1], (BLK, tok)) for at in range(RB, tok // BLK)]
    table_ref[TABLE:] = jnp.where(past, NEG, jnp.concatenate(tail, axis=0))
    for h in range(HEADS):
        q, k, v, g = (ref[:, cols(h)] for ref in (q_ref, k_ref, v_ref, g_ref))
        top, p = own_exps(nt(k, q), table_ref)
        prod = nt(v, g)
        p_ref[h], prod_ref[h] = p, prod
        stats_ref[h] = rows_of(sums_of(top, p, prod))


def first_kernel(q_ref, g_ref, x_ref, table_ref, stats_ref, p_ref, prod_ref):
    for h in range(SPLIT):
        q, g = q_ref[:, cols(h)], g_ref[:, cols(h)]
        top, p = exps_of(nt(x_ref[0, :, cols(h)], q), table_ref, 8)
        prod = nt(x_ref[1, :, cols(h)], g)
        p_ref[h], prod_ref[h] = p, prod
        stats_ref[h] = rows_of(sums_of(top, p, prod))


def rim_kernel(first, q_ref, g_ref, x_ref, i_ref, table_ref, stats_ref, *refs):
    gx_ref, final_ref, ds_ref, pi_ref, prodi_ref = refs[-5:]
    heads = range(x_ref.shape[2] // DEPTH)
    parts = []
    for at in heads:
        h = first + at
        q, g = q_ref[:, cols(h)], g_ref[:, cols(h)]
        top, p = exps_of(nt(i_ref[0, :, cols(h)], q), table_ref, 8 + RB)
        prod = nt(i_ref[1, :, cols(h)], g)
        pi_ref[at], prodi_ref[at] = p, prod
        part_i = sums_of(top, p, prod)
        if first:
            top, p = exps_of(nt(x_ref[0, :, cols(at)], q), table_ref, 8)
            prod = nt(x_ref[1, :, cols(at)], g)
            part_x = sums_of(top, p, prod)
        else:
            stats_x_ref, px_ref, prodx_ref = refs[:3]
            part_x, p, prod = known(stats_x_ref.at[h]), px_ref[h], prodx_ref[h]
        parts.append((part_i, part_x, p, prod))
    for at, (part_i, part_x, p, prod) in zip(heads, parts):
        h = first + at
        q, g = q_ref[:, cols(h)], g_ref[:, cols(h)]
        own = known(stats_ref.at[h])
        top, total, raw = merged(merged(own, part_i), part_x)
        inv = jnp.where(total > 0.0, 1.0 / jnp.where(total > 0.0, total, 1.0), 0.0)
        delta = raw * inv
        w, ds = grads_of(p, prod, jnp.exp2(part_x[0] - top) * inv, delta)
        gx_ref[0, :, cols(at)] = nn(ds, q).astype(jnp.bfloat16)
        gx_ref[1, :, cols(at)] = nn(w, g).astype(jnp.bfloat16)
        ds_ref[at] = ds
        final_ref[at] = rows_of((jnp.exp2(own[0] - top) * inv, jnp.exp2(part_i[0] - top) * inv, delta))


def inside_kernel(q_ref, g_ref, *refs):
    gi_ref, ds_ref = refs[-2:]
    for h in range(HEADS):
        final_ref, pi_ref, prodi_ref = refs[:3] if h < SPLIT else refs[3:6]
        at = h if h < SPLIT else h - SPLIT
        q, g = q_ref[:, cols(h)], g_ref[:, cols(h)]
        w, ds = grads_of(pi_ref[at], prodi_ref[at], final_ref[at, 1:2], final_ref[at, 2:3])
        gi_ref[0, :, cols(h)] = nn(ds, q).astype(jnp.bfloat16)
        gi_ref[1, :, cols(h)] = nn(w, g).astype(jnp.bfloat16)
        ds_ref[h] = ds


def rest_of(first, at, q_ref, k_ref, g_ref, p_ref, prod_ref, final_ref, x_ref, dsx_ref, i_ref, dsi_ref):
    h = first + at
    q, k, g = (ref[:, cols(h)] for ref in (q_ref, k_ref, g_ref))
    w, ds = grads_of(p_ref[h], prod_ref[h], final_ref[at, 0:1], final_ref[at, 2:3])
    frame_k = jnp.concatenate([k, x_ref[0, :, cols(at)], i_ref[0, :, cols(h)]], axis=0)
    dq = tn(frame_k, jnp.concatenate([ds, dsx_ref[at], dsi_ref[h]], axis=0))
    return dq.T.astype(jnp.bfloat16), nn(ds, q), nn(w, g)


def held_kernel(first, *refs):
    _, dq_ref, pk_ref, pv_ref, dq_buf, sems = refs[10:]
    copies = []
    for at in range(pk_ref.shape[1] // DEPTH):
        dq, pk_ref[:, cols(at)], pv_ref[:, cols(at)] = rest_of(first, at, *refs[:10])
        dq_buf[:, cols(at)] = dq
        copies.append(pltpu.make_async_copy(dq_buf.at[:, cols(at)], dq_ref.at[:, cols(first + at)], sems.at[at]))
        copies[-1].start()
    for copy in copies:
        copy.wait()


def done_kernel(first, *refs):
    gx_ref, gi_ref, _, dq_ref, dk_ref, dv_ref, dq_buf, dk_buf, dv_buf, sems = refs[10:]
    copies = []
    for at in range(dq_buf.shape[1] // DEPTH):
        dq, dk, dv = rest_of(first, at, *refs[:10])
        dq_buf[:, cols(at)] = dq
        for slot, buf, part in ((0, dk_buf, dk), (1, dv_buf, dv)):
            lead = gx_ref[slot, :, cols(at)].astype(jnp.float32) + gi_ref[slot, :, cols(first + at)].astype(jnp.float32)
            buf[:RIM, cols(at)] = (part[:RIM] + lead).astype(jnp.bfloat16)
            buf[RIM:, cols(at)] = part[RIM:].astype(jnp.bfloat16)
        for n, (buf, out) in enumerate(((dq_buf, dq_ref), (dk_buf, dk_ref), (dv_buf, dv_ref))):
            copies.append(pltpu.make_async_copy(buf.at[:, cols(at)], out.at[:, cols(first + at)], sems.at[n, at]))
            copies[-1].start()
    for copy in copies:
        copy.wait()


def add_kernel(first, pk_ref, pv_ref, gx_ref, gi_ref, _k, _v, dk_ref, dv_ref, dk_buf, dv_buf, sems):
    copies = []
    for at in range(pk_ref.shape[1] // DEPTH):
        for slot, (own, buf, out) in enumerate(((pk_ref, dk_buf, dk_ref), (pv_ref, dv_buf, dv_ref))):
            lead = gx_ref[slot, :, cols(at)].astype(jnp.float32) + gi_ref[slot, :, cols(first + at)].astype(jnp.float32)
            buf[:RIM, cols(at)] = (own[:RIM, cols(at)] + lead).astype(jnp.bfloat16)
            buf[RIM:, cols(at)] = own[RIM:, cols(at)].astype(jnp.bfloat16)
            copies.append(pltpu.make_async_copy(buf.at[:, cols(at)], out.at[:, cols(first + at)], sems.at[slot, at]))
            copies[-1].start()
    for copy in copies:
        copy.wait()


VMEM = pl.BlockSpec(memory_space=pltpu.VMEM)
HBM = pl.BlockSpec(memory_space=pltpu.HBM)
ANY = pl.BlockSpec(memory_space=pl.ANY)


def call(body, name, ins, outs, out_specs, args, scratch=(), alias=None, limit=24):
    return pl.pallas_call(
        body,
        in_specs=ins,
        out_specs=out_specs,
        out_shape=outs,
        scratch_shapes=scratch,
        input_output_aliases=alias or {},
        compiler_params=pltpu.CompilerParams(vmem_limit_bytes=int(limit * MIB)),
        cost_estimate=pl.CostEstimate(flops=WEIGHT[name] * MEGA, bytes_accessed=1000, transcendentals=0),
        name=name,
    )(*args)


def shape(*dims, dtype=jnp.bfloat16):
    return jax.ShapeDtypeStruct(dims, dtype)


def on_device(queries, keys, values, out_grad, band_counts, block_lists, slot_counts):
    tok, width = queries.shape
    f32 = functools.partial(shape, dtype=jnp.float32)
    cuts = ((0, SPLIT), (SPLIT, HEADS))
    part = HEADS - SPLIT
    q, k, v, g = queries, keys, values, out_grad
    lead_a, lead_b = call(
        load_kernel,
        "load_bands",
        [HBM] * 2,
        [shape(2, RIM, SPLIT * DEPTH), shape(2, RIM, part * DEPTH)],
        [VMEM] * 2,
        (keys, values),
        [pltpu.SemaphoreType.DMA((4,))],
        limit=LOAD_LIMIT,
    )
    x_a, x_b = swap_across(lead_a), swap_across(lead_b)
    lead_i = call(pack_kernel, "pack_leads", [VMEM] * 2, shape(2, RIM, width), VMEM, (k, v))
    i = swap_inside(lead_i)
    table, stats, p, prod = call(
        own_kernel,
        "own_stats",
        [VMEM] * 7,
        [f32(TABLE + tok - RIM, tok), f32(HEADS, 8, tok), f32(HEADS, tok, tok), f32(HEADS, tok, tok)],
        [VMEM] * 4,
        (band_counts[:, None], slot_counts[None], block_lists, q, k, v, g),
    )
    stats_x, px, prodx = call(
        first_kernel,
        "first_stats",
        [VMEM] * 4,
        [f32(SPLIT, 8, tok), f32(SPLIT, RIM, tok), f32(SPLIT, RIM, tok)],
        [VMEM] * 3,
        (q, g, x_a, table),
    )

    def rim(first, x, *more):
        heads = x.shape[2] // DEPTH
        return call(
            functools.partial(rim_kernel, first),
            "rim_grads",
            [VMEM] * (6 + len(more)),
            [shape(*x.shape), f32(heads, 8, tok), shape(heads, RIM, tok), f32(heads, RIM, tok), f32(heads, RIM, tok)],
            [VMEM] * 5,
            (q, g, x, i, table, stats) + more,
        )

    gx_a, final_a, dsx_a, *inside_a = rim(0, x_a, stats_x, px, prodx)
    gx_a = swap_across(gx_a)
    gx_b, final_b, dsx_b, *inside_b = rim(SPLIT, x_b)
    gx_b = swap_across(gx_b)
    gi, ds_i = call(
        inside_kernel,
        "inside_grads",
        [VMEM] * 8,
        [shape(2, RIM, width), shape(HEADS, RIM, tok)],
        [VMEM] * 2,
        (q, g, final_a, *inside_a, final_b, *inside_b),
    )
    gi = swap_inside(gi)

    dq, pk, pv = call(
        functools.partial(held_kernel, SPLIT),
        "held_grads",
        [VMEM] * 10 + [ANY],
        [shape(tok, width), f32(tok, part * DEPTH), f32(tok, part * DEPTH)],
        [ANY, VMEM, VMEM],
        (q, k, g, p, prod, final_b, x_b, dsx_b, i, ds_i, gx_a),
        [pltpu.VMEM((tok, part * DEPTH), jnp.bfloat16), pltpu.SemaphoreType.DMA((part,))],
    )
    dq, dk, dv = call(
        functools.partial(done_kernel, 0),
        "done_grads",
        [VMEM] * 12 + [ANY],
        [shape(tok, width)] * 3,
        [ANY] * 3,
        (q, k, g, p, prod, final_a, x_a, dsx_a, i, ds_i, gx_a, gi, dq),
        [pltpu.VMEM((tok, SPLIT * DEPTH), jnp.bfloat16)] * 3 + [pltpu.SemaphoreType.DMA((3, SPLIT))],
        {12: 0},
    )
    dk, dv = call(
        functools.partial(add_kernel, SPLIT),
        "add_rims",
        [VMEM] * 4 + [ANY] * 2,
        [shape(tok, width)] * 2,
        [ANY] * 2,
        (pk, pv, gx_b, gi, dk, dv),
        [pltpu.VMEM((tok, part * DEPTH), jnp.bfloat16)] * 2 + [pltpu.SemaphoreType.DMA((2, part))],
        {4: 0, 5: 1},
    )
    return dq, dk, dv


def solution(mesh):
    placed = P(("member", "band"), None)
    flat = P(("member", "band"))
    return jax.shard_map(
        on_device,
        mesh=mesh,
        in_specs=(placed, placed, placed, placed, flat, placed, flat),
        out_specs=(placed, placed, placed),
        check_vma=False,
    )
```

```python
import functools
import jax
import jax.numpy as jnp
from jax import lax
from jax.experimental import pallas as pl
from jax.experimental.pallas import tpu as pltpu
from jax.sharding import PartitionSpec as P

HEADS = 8
DEPTH = 128
BLK = 32
RB = 6
RIM = RB * BLK
TABLE = 32
LOG2E = 1.4426950408889634
NEG = -1e30
FLOOR = -1e20
MIB = 1024 * 1024
LOAD_LIMIT = 53.5
SPLIT = 4
SENT = 1
PIECES = 2 // SENT
STATS = 32
MEGA = 10**6
WEIGHT = {
    "load_bands": 5500,
    "pack_leads": 1,
    "pack_inside": 1,
    "own_stats": 1,
    "first_stats": 11000,
    "rim_grads": 1,
    "inside_grads": 1,
    "rest_grads": 11000,
    "done_grads": 11000,
    "add_rims": 1,
}


def nt(a, b):
    return lax.dot_general(a, b, (((1,), (1,)), ((), ())), preferred_element_type=jnp.float32)


def tn(a, b):
    return lax.dot_general(a, b, (((0,), (0,)), ((), ())), preferred_element_type=jnp.float32)


def nn(a, b):
    return jnp.dot(a, b, preferred_element_type=jnp.float32)


def cols(h):
    return slice(h * DEPTH, (h + 1) * DEPTH)


SCALE = DEPTH ** -0.5 * LOG2E


def exps_of(score, bias, first):
    parts = [score[at * BLK : (at + 1) * BLK] for at in range(score.shape[0] // BLK)]
    rows = [bias[first + at : first + at + 1, :] for at in range(len(parts))]
    tops = [jnp.max(part, axis=0, keepdims=True) * SCALE + row for part, row in zip(parts, rows)]
    top = functools.reduce(jnp.maximum, tops, jnp.full_like(tops[0], FLOOR))
    return top, jnp.concatenate([jnp.exp2(part * SCALE + (row - top)) for part, row in zip(parts, rows)], axis=0)


def own_exps(score, bias):
    lead, tail = score[:RIM], score[RIM:] * SCALE + bias[TABLE:, :]
    parts = [lead[at * BLK : (at + 1) * BLK] for at in range(RB)]
    rows = [bias[at : at + 1, :] for at in range(RB)]
    tops = [jnp.max(part, axis=0, keepdims=True) * SCALE + row for part, row in zip(parts, rows)]
    top = functools.reduce(jnp.maximum, tops, jnp.maximum(jnp.max(tail, axis=0, keepdims=True), FLOOR))
    exps = [jnp.exp2(part * SCALE + (row - top)) for part, row in zip(parts, rows)]
    return top, jnp.concatenate(exps + [jnp.exp2(tail - top)], axis=0)


def table_of(lists, live, ids, count, tok):
    blocks, slots = lists.shape
    hit = jnp.zeros((blocks, ids.shape[1]), jnp.float32)
    for l in range(slots):
        hit = jnp.where((lists[:, l : l + 1] == ids) & (live > l), 1.0, hit)
    lane = lax.broadcasted_iota(jnp.int32, (blocks, tok), 1)
    row = lax.broadcasted_iota(jnp.int32, (blocks, tok), 0)
    spread = jnp.where((lane // BLK == row) & (lane < count), 1.0, 0.0)
    return jnp.where(tn(hit, spread) > 0.5, 0.0, NEG)


def merged(a, b):
    top = jnp.maximum(a[0], b[0])
    fa, fb = jnp.exp2(a[0] - top), jnp.exp2(b[0] - top)
    return top, a[1] * fa + b[1] * fb, a[2] * fa + b[2] * fb


def sums_of(top, p, prod):
    return top, jnp.sum(p, axis=0, keepdims=True), jnp.sum(p * prod, axis=0, keepdims=True)


def rows_of(values):
    pad = jnp.zeros((8 - len(values), values[0].shape[1]), jnp.float32)
    return jnp.concatenate(tuple(values) + (pad,), axis=0)


def known(ref):
    return ref[0:1], ref[1:2], ref[2:3]


def thirds_of(rows):
    high = rows.astype(jnp.bfloat16)
    left = rows - high.astype(jnp.float32)
    middle = left.astype(jnp.bfloat16)
    low = (left - middle.astype(jnp.float32)).astype(jnp.bfloat16)
    parts = [part.astype(jnp.float32) for part in (high, middle, low)]
    return jnp.concatenate(parts + [jnp.zeros_like(rows)], axis=0).astype(jnp.bfloat16)


def whole_of(parts):
    high, middle, low = (parts[at * 8 : (at + 1) * 8] for at in range(3))
    return high + (middle + low)


def grads_of(p, prod, factor, delta):
    w = (p * factor).astype(jnp.bfloat16)
    ds = (p * (factor * (DEPTH ** -0.5)) * (prod - delta)).astype(jnp.bfloat16)
    return w, ds


def swap_across(x):
    count = lax.axis_size("band")
    pairs = [(at, at + 1) for at in range(1, count - 1, 2)]
    return lax.ppermute(x, "band", pairs + [(b, a) for a, b in pairs])


def swap_inside(x):
    return lax.ppermute(x, "band", [(at, at ^ 1) for at in range(lax.axis_size("band"))])


def load_kernel(k_ref, v_ref, lead_ref, sems):
    copies = [
        pltpu.make_async_copy(
            src.at[pl.ds(0, RIM), pl.ds(0, SPLIT * DEPTH)], lead_ref.at[pl.ds(at * RIM, RIM), :], sems.at[at]
        )
        for at, src in enumerate((k_ref, v_ref))
    ]
    for copy in copies:
        copy.start()
    for copy in copies:
        copy.wait()


def pack_kernel(k_ref, v_ref, q_ref, g_ref, lead_ref):
    for at, ref in enumerate((k_ref, v_ref)):
        lead_ref[at * RIM : (at + 1) * RIM, :] = ref[:RIM, SPLIT * DEPTH :]
    rows = q_ref.shape[0] // PIECES
    for at, ref in enumerate((q_ref, g_ref)):
        for n in range(SENT):
            for piece in range(PIECES):
                part = ref[piece * rows : (piece + 1) * rows, cols(HEADS - SENT + n)]
                lead_ref[2 * RIM :, cols(2 * at + n * PIECES + piece)] = part


def sent_of(x_ref, at, n):
    parts = [x_ref[2 * RIM :, cols(2 * at + n * PIECES + piece)] for piece in range(PIECES)]
    return jnp.concatenate(parts, axis=0)


def inside_pack_kernel(k_ref, v_ref, _, lead_ref):
    for at, ref in enumerate((k_ref, v_ref)):
        lead_ref[at] = ref[:RIM, :]


def own_kernel(count_ref, live_ref, lists_ref, q_ref, k_ref, v_ref, g_ref, table_ref, stats_ref, p_ref, prod_ref):
    tok = q_ref.shape[0]
    blocks = lists_ref.shape[0]
    count = count_ref[...]
    row = lax.broadcasted_iota(jnp.int32, (blocks, blocks), 0)
    lane = lax.broadcasted_iota(jnp.int32, (blocks, blocks), 1)
    live = jnp.sum(jnp.where(row == lane, live_ref[...], 0), axis=1, keepdims=True)
    odd = lax.axis_index("band") % 2
    slot = lax.broadcasted_iota(jnp.int32, (blocks, TABLE), 1)
    x_first = 8 + RB * odd
    i_first = 8 + RB * (1 - odd)
    ids = jnp.where(slot < 8, slot, jnp.where(slot < 8 + RB, slot - 8 + x_first, slot - 8 - RB + i_first))
    ids = jnp.where(slot < 8 + 2 * RB, ids, -1)
    table = table_of(lists_ref[...], live, ids, count, tok)
    table_ref[:TABLE] = table
    past = lax.broadcasted_iota(jnp.int32, (tok - RIM, tok), 0) + RIM >= count
    tail = [jnp.broadcast_to(table[at : at + 1], (BLK, tok)) for at in range(RB, tok // BLK)]
    table_ref[TABLE:] = jnp.where(past, NEG, jnp.concatenate(tail, axis=0))
    for h in range(HEADS):
        q, k, v, g = (ref[:, cols(h)] for ref in (q_ref, k_ref, v_ref, g_ref))
        top, p = own_exps(nt(k, q), table_ref)
        prod = nt(v, g)
        p_ref[h], prod_ref[h] = p, prod
        stats_ref[h] = rows_of(sums_of(top, p, prod))


def first_kernel(q_ref, g_ref, x_ref, table_ref, stats_ref, p_ref, prod_ref):
    for h in range(SPLIT):
        q, g = q_ref[:, cols(h)], g_ref[:, cols(h)]
        top, p = exps_of(nt(x_ref[:RIM, cols(h)], q), table_ref, 8)
        prod = nt(x_ref[RIM : 2 * RIM, cols(h)], g)
        p_ref[h], prod_ref[h] = p, prod
        stats_ref[h] = rows_of(sums_of(top, p, prod))


def rim_kernel(first, q_ref, g_ref, x_ref, i_ref, table_ref, stats_ref, *refs):
    gx_ref, final_ref, ds_ref, pi_ref, prodi_ref = refs[-5:]
    heads = range(x_ref.shape[1] // DEPTH)
    returned = len(heads) - (SENT if first else 0)
    parts = []
    for at in heads:
        h = first + at
        q, g = q_ref[:, cols(h)], g_ref[:, cols(h)]
        top, p = exps_of(nt(i_ref[0, :, cols(h)], q), table_ref, 8 + RB)
        prod = nt(i_ref[1, :, cols(h)], g)
        pi_ref[at], prodi_ref[at] = p, prod
        part_i = sums_of(top, p, prod)
        if first:
            top, p = exps_of(nt(x_ref[:RIM, cols(at)], q), table_ref, 8)
            prod = nt(x_ref[RIM : 2 * RIM, cols(at)], g)
            part_x = sums_of(top, p, prod)
        else:
            stats_x_ref, px_ref, prodx_ref = refs[:3]
            part_x, p, prod = known(stats_x_ref.at[h]), px_ref[h], prodx_ref[h]
        parts.append((part_i, part_x, p, prod))
    for at, (part_i, part_x, p, prod) in zip(heads, parts):
        h = first + at
        q, g = q_ref[:, cols(h)], g_ref[:, cols(h)]
        own = known(stats_ref.at[h])
        top, total, raw = merged(merged(own, part_i), part_x)
        inv = jnp.where(total > 0.0, 1.0 / jnp.where(total > 0.0, total, 1.0), 0.0)
        delta = raw * inv
        w, ds = grads_of(p, prod, jnp.exp2(part_x[0] - top) * inv, delta)
        if at < returned:
            gx_ref[:RIM, cols(at)] = nn(ds, q).astype(jnp.bfloat16)
            gx_ref[RIM : 2 * RIM, cols(at)] = nn(w, g).astype(jnp.bfloat16)
        else:
            rows = jnp.concatenate([table_ref[8 : 8 + RB] - top, inv, delta], axis=0)
            begin = 2 * RIM + (at - returned) * STATS
            gx_ref[begin : begin + STATS, : rows.shape[1]] = thirds_of(rows)
        ds_ref[at] = ds
        final_ref[at] = rows_of((jnp.exp2(own[0] - top) * inv, jnp.exp2(part_i[0] - top) * inv, delta))


def inside_kernel(q_ref, g_ref, *refs):
    gi_ref, ds_ref = refs[-2:]
    for h in range(HEADS):
        final_ref, pi_ref, prodi_ref = refs[:3] if h < SPLIT else refs[3:6]
        at = h if h < SPLIT else h - SPLIT
        q, g = q_ref[:, cols(h)], g_ref[:, cols(h)]
        w, ds = grads_of(pi_ref[at], prodi_ref[at], final_ref[at, 1:2], final_ref[at, 2:3])
        gi_ref[0, :, cols(h)] = nn(ds, q).astype(jnp.bfloat16)
        gi_ref[1, :, cols(h)] = nn(w, g).astype(jnp.bfloat16)
        ds_ref[h] = ds


def rest_kernel(q_ref, k_ref, v_ref, g_ref, p_ref, prod_ref, i_ref, dsi_ref, *refs):
    parts, (_, dq_ref, pk_ref, pv_ref, score_ref, products_ref) = (refs[:3], refs[3:6]), refs[6:]
    x_ref = parts[1][1]
    for n in range(SENT):
        h = HEADS - SENT + n
        score_ref[n] = nt(k_ref[:RIM, cols(h)], sent_of(x_ref, 0, n))
        products_ref[n] = nt(v_ref[:RIM, cols(h)], sent_of(x_ref, 1, n))
    for h in range(HEADS):
        at = h if h < SPLIT else h - SPLIT
        final_ref, x_ref, dsx_ref = parts[0] if h < SPLIT else parts[1]
        q, k, g = (ref[:, cols(h)] for ref in (q_ref, k_ref, g_ref))
        w, ds = grads_of(p_ref[h], prod_ref[h], final_ref[at, 0:1], final_ref[at, 2:3])
        pk_ref[:, cols(h)] = nn(ds, q)
        pv_ref[:, cols(h)] = nn(w, g)
        frame_k = jnp.concatenate([k, x_ref[:RIM, cols(at)], i_ref[0, :, cols(h)]], axis=0)
        dq = tn(frame_k, jnp.concatenate([ds, dsx_ref[at], dsi_ref[h]], axis=0))
        dq_ref[:, cols(h)] = dq.T.astype(jnp.bfloat16)


def summed(own_ref, lead, gi_ref, slot, h):
    lead = own_ref[:RIM, cols(h)] + (lead + gi_ref[slot, :, cols(h)].astype(jnp.float32))
    return jnp.concatenate([lead, own_ref[RIM:, cols(h)]], axis=0).astype(jnp.bfloat16)


def done_kernel(dq_in, pk_ref, pv_ref, gx_ref, gi_ref, dq_ref, dk_ref, dv_ref, dk_buf, dv_buf, sems):
    span = pl.ds(0, dk_buf.shape[1])
    copies = [
        pltpu.make_async_copy(dq_in, dq_ref, sems.at[0]),
        pltpu.make_async_copy(dk_buf, dk_ref.at[:, span], sems.at[1]),
        pltpu.make_async_copy(dv_buf, dv_ref.at[:, span], sems.at[2]),
    ]
    copies[0].start()
    for slot, (own, buf) in enumerate(((pk_ref, dk_buf), (pv_ref, dv_buf))):
        for h in range(SPLIT):
            lead = gx_ref[slot * RIM : (slot + 1) * RIM, cols(h)].astype(jnp.float32)
            buf[:, cols(h)] = summed(own, lead, gi_ref, slot, h)
        copies[1 + slot].start()
    for copy in copies:
        copy.wait()


def add_kernel(pk_ref, pv_ref, gx_ref, gi_ref, x_ref, score_ref, prod_ref, _k, _v, dk_ref, dv_ref, dk_buf, dv_buf, sems):
    heads = HEADS - SPLIT
    returned = heads - SENT
    leads = {}
    for n in range(SENT):
        begin = 2 * RIM + n * STATS
        rows = whole_of(gx_ref[begin : begin + STATS, : score_ref.shape[2]].astype(jnp.float32))
        blocks = [jnp.exp2(score_ref[n, e * BLK : (e + 1) * BLK] * SCALE + rows[e : e + 1]) for e in range(RB)]
        w, ds = grads_of(jnp.concatenate(blocks, axis=0), prod_ref[n], rows[RB : RB + 1], rows[RB + 1 : RB + 2])
        leads[returned + n] = nn(ds, sent_of(x_ref, 0, n)), nn(w, sent_of(x_ref, 1, n))
    span = pl.ds(SPLIT * DEPTH, heads * DEPTH)
    copies = [
        pltpu.make_async_copy(buf, out.at[:, span], sems.at[slot])
        for slot, (buf, out) in enumerate(((dk_buf, dk_ref), (dv_buf, dv_ref)))
    ]
    for slot, (own, buf) in enumerate(((pk_ref, dk_buf), (pv_ref, dv_buf))):
        for at in range(heads):
            if at in leads:
                lead = leads[at][slot]
            else:
                lead = gx_ref[slot * RIM : (slot + 1) * RIM, cols(at)].astype(jnp.float32)
            buf[:, cols(at)] = summed(own, lead, gi_ref, slot, SPLIT + at)
        copies[slot].start()
    for copy in copies:
        copy.wait()


VMEM = pl.BlockSpec(memory_space=pltpu.VMEM)
HBM = pl.BlockSpec(memory_space=pltpu.HBM)
ANY = pl.BlockSpec(memory_space=pl.ANY)


def call(body, name, ins, outs, out_specs, args, scratch=(), alias=None, limit=24):
    return pl.pallas_call(
        body,
        in_specs=ins,
        out_specs=out_specs,
        out_shape=outs,
        scratch_shapes=scratch,
        input_output_aliases=alias or {},
        compiler_params=pltpu.CompilerParams(vmem_limit_bytes=int(limit * MIB)),
        cost_estimate=pl.CostEstimate(flops=WEIGHT[name] * MEGA, bytes_accessed=1000, transcendentals=0),
        name=name,
    )(*args)


def shape(*dims, dtype=jnp.bfloat16):
    return jax.ShapeDtypeStruct(dims, dtype)


def on_device(queries, keys, values, out_grad, band_counts, block_lists, slot_counts):
    tok, width = queries.shape
    f32 = functools.partial(shape, dtype=jnp.float32)
    cuts = ((0, SPLIT), (SPLIT, HEADS))
    part = HEADS - SPLIT
    q, k, v, g = queries, keys, values, out_grad
    lead_a = call(
        load_kernel,
        "load_bands",
        [HBM] * 2,
        shape(2 * RIM, SPLIT * DEPTH),
        VMEM,
        (k, v),
        [pltpu.SemaphoreType.DMA((2,))],
        limit=LOAD_LIMIT,
    )
    lead_b = call(pack_kernel, "pack_leads", [VMEM] * 4, shape(2 * RIM + tok // PIECES, part * DEPTH), VMEM, (k, v, q, g))
    x_a, x_b = swap_across(lead_a), swap_across(lead_b)
    lead_i = call(inside_pack_kernel, "pack_inside", [VMEM] * 2 + [ANY], shape(2, RIM, width), VMEM, (k, v, lead_b))
    i = swap_inside(lead_i)
    table, stats, p, prod = call(
        own_kernel,
        "own_stats",
        [VMEM] * 7,
        [f32(TABLE + tok - RIM, tok), f32(HEADS, 8, tok), f32(HEADS, tok, tok), f32(HEADS, tok, tok)],
        [VMEM] * 4,
        (band_counts[:, None], slot_counts[None], block_lists, q, k, v, g),
    )
    stats_x, px, prodx = call(
        first_kernel,
        "first_stats",
        [VMEM] * 4,
        [f32(SPLIT, 8, tok), f32(SPLIT, RIM, tok), f32(SPLIT, RIM, tok)],
        [VMEM] * 3,
        (q, g, x_a, table),
    )

    def rim(first, x, *more):
        heads = x.shape[1] // DEPTH
        gx = (2 * RIM + SENT * STATS, (heads - SENT) * DEPTH) if first else x.shape
        return call(
            functools.partial(rim_kernel, first),
            "rim_grads",
            [VMEM] * (6 + len(more)),
            [shape(*gx), f32(heads, 8, tok), shape(heads, RIM, tok), f32(heads, RIM, tok), f32(heads, RIM, tok)],
            [VMEM] * 5,
            (q, g, x, i, table, stats) + more,
        )

    gx_a, final_a, dsx_a, *inside_a = rim(0, x_a, stats_x, px, prodx)
    gx_a = swap_across(gx_a)
    gx_b, final_b, dsx_b, *inside_b = rim(SPLIT, x_b)
    gx_b = swap_across(gx_b)
    gi, ds_i = call(
        inside_kernel,
        "inside_grads",
        [VMEM] * 8,
        [shape(2, RIM, width), shape(HEADS, RIM, tok)],
        [VMEM] * 2,
        (q, g, final_a, *inside_a, final_b, *inside_b),
    )
    gi = swap_inside(gi)

    dq, pk, pv, score, products = call(
        rest_kernel,
        "rest_grads",
        [VMEM] * 14 + [ANY],
        [shape(tok, width), f32(tok, width), f32(tok, width), f32(SENT, RIM, tok), f32(SENT, RIM, tok)],
        [VMEM] * 5,
        (q, k, v, g, p, prod, i, ds_i, final_a, x_a, dsx_a, final_b, x_b, dsx_b, gx_a),
    )
    dq, dk, dv = call(
        done_kernel,
        "done_grads",
        [VMEM] * 5,
        [shape(tok, width)] * 3,
        [ANY] * 3,
        (dq, pk, pv, gx_a, gi),
        [pltpu.VMEM((tok, SPLIT * DEPTH), jnp.bfloat16)] * 2 + [pltpu.SemaphoreType.DMA((3,))],
    )
    dk, dv = call(
        add_kernel,
        "add_rims",
        [VMEM] * 7 + [ANY] * 2,
        [shape(tok, width)] * 2,
        [ANY] * 2,
        (pk, pv, gx_b, gi, x_b, score, products, dk, dv),
        [pltpu.VMEM((tok, part * DEPTH), jnp.bfloat16)] * 2 + [pltpu.SemaphoreType.DMA((2,))],
        {7: 0, 8: 1},
    )
    return dq, dk, dv


def solution(mesh):
    placed = P(("member", "band"), None)
    flat = P(("member", "band"))
    return jax.shard_map(
        on_device,
        mesh=mesh,
        in_specs=(placed, placed, placed, placed, flat, placed, flat),
        out_specs=(placed, placed, placed),
        check_vma=False,
    )
```

```python
import functools
import jax
import jax.numpy as jnp
from jax import lax
from jax.experimental import pallas as pl
from jax.experimental.pallas import tpu as pltpu
from jax.sharding import PartitionSpec as P

HEADS = 8
DEPTH = 128
BLK = 32
RB = 6
RIM = RB * BLK
TABLE = 32
LOG2E = 1.4426950408889634
NEG = -1e30
FLOOR = -1e20
MIB = 1024 * 1024
LOAD_LIMIT = 53.5
SPLIT = 4
SENT = 2
PIECES = 2
STATS = 32
MEGA = 10**6
WEIGHT = {
    "load_bands": 5500,
    "pack_leads": 1,
    "pack_inside": 1,
    "own_stats": 1,
    "first_stats": 11000,
    "rim_grads": 1,
    "inside_grads": 1,
    "rest_grads": 11000,
    "done_grads": 11000,
    "add_rims": 1,
}


def nt(a, b):
    return lax.dot_general(a, b, (((1,), (1,)), ((), ())), preferred_element_type=jnp.float32)


def tn(a, b):
    return lax.dot_general(a, b, (((0,), (0,)), ((), ())), preferred_element_type=jnp.float32)


def nn(a, b):
    return jnp.dot(a, b, preferred_element_type=jnp.float32)


def cols(h):
    return slice(h * DEPTH, (h + 1) * DEPTH)


SCALE = DEPTH ** -0.5 * LOG2E


def exps_of(score, bias, first):
    parts = [score[at * BLK : (at + 1) * BLK] for at in range(score.shape[0] // BLK)]
    rows = [bias[first + at : first + at + 1, :] for at in range(len(parts))]
    tops = [jnp.max(part, axis=0, keepdims=True) * SCALE + row for part, row in zip(parts, rows)]
    top = functools.reduce(jnp.maximum, tops, jnp.full_like(tops[0], FLOOR))
    return top, jnp.concatenate([jnp.exp2(part * SCALE + (row - top)) for part, row in zip(parts, rows)], axis=0)


def own_exps(score, bias):
    lead, tail = score[:RIM], score[RIM:] * SCALE + bias[TABLE:, :]
    parts = [lead[at * BLK : (at + 1) * BLK] for at in range(RB)]
    rows = [bias[at : at + 1, :] for at in range(RB)]
    tops = [jnp.max(part, axis=0, keepdims=True) * SCALE + row for part, row in zip(parts, rows)]
    top = functools.reduce(jnp.maximum, tops, jnp.maximum(jnp.max(tail, axis=0, keepdims=True), FLOOR))
    exps = [jnp.exp2(part * SCALE + (row - top)) for part, row in zip(parts, rows)]
    return top, jnp.concatenate(exps + [jnp.exp2(tail - top)], axis=0)


def table_of(lists, live, ids, count, tok):
    blocks, slots = lists.shape
    hit = jnp.zeros((blocks, ids.shape[1]), jnp.float32)
    for l in range(slots):
        hit = jnp.where((lists[:, l : l + 1] == ids) & (live > l), 1.0, hit)
    lane = lax.broadcasted_iota(jnp.int32, (blocks, tok), 1)
    row = lax.broadcasted_iota(jnp.int32, (blocks, tok), 0)
    spread = jnp.where((lane // BLK == row) & (lane < count), 1.0, 0.0)
    return jnp.where(tn(hit, spread) > 0.5, 0.0, NEG)


def merged(a, b):
    top = jnp.maximum(a[0], b[0])
    fa, fb = jnp.exp2(a[0] - top), jnp.exp2(b[0] - top)
    return top, a[1] * fa + b[1] * fb, a[2] * fa + b[2] * fb


def sums_of(top, p, prod):
    return top, jnp.sum(p, axis=0, keepdims=True), jnp.sum(p * prod, axis=0, keepdims=True)


def rows_of(values):
    pad = jnp.zeros((8 - len(values), values[0].shape[1]), jnp.float32)
    return jnp.concatenate(tuple(values) + (pad,), axis=0)


def known(ref):
    return ref[0:1], ref[1:2], ref[2:3]


def thirds_of(rows):
    high = rows.astype(jnp.bfloat16)
    left = rows - high.astype(jnp.float32)
    middle = left.astype(jnp.bfloat16)
    low = (left - middle.astype(jnp.float32)).astype(jnp.bfloat16)
    parts = [part.astype(jnp.float32) for part in (high, middle, low)]
    return jnp.concatenate(parts + [jnp.zeros_like(rows)], axis=0).astype(jnp.bfloat16)


def whole_of(parts):
    high, middle, low = (parts[at * 8 : (at + 1) * 8] for at in range(3))
    return high + (middle + low)


def grads_of(p, prod, factor, delta):
    w = (p * factor).astype(jnp.bfloat16)
    ds = (p * (factor * (DEPTH ** -0.5)) * (prod - delta)).astype(jnp.bfloat16)
    return w, ds


def swap_across(x):
    count = lax.axis_size("band")
    pairs = [(at, at + 1) for at in range(1, count - 1, 2)]
    return lax.ppermute(x, "band", pairs + [(b, a) for a, b in pairs])


def swap_inside(x):
    return lax.ppermute(x, "band", [(at, at ^ 1) for at in range(lax.axis_size("band"))])


def load_kernel(k_ref, v_ref, lead_ref, sems):
    copies = [
        pltpu.make_async_copy(
            src.at[pl.ds(0, RIM), pl.ds(0, SPLIT * DEPTH)], lead_ref.at[pl.ds(at * RIM, RIM), :], sems.at[at]
        )
        for at, src in enumerate((k_ref, v_ref))
    ]
    for copy in copies:
        copy.start()
    for copy in copies:
        copy.wait()


def pack_kernel(k_ref, v_ref, q_ref, g_ref, lead_ref):
    for at, ref in enumerate((k_ref, v_ref)):
        lead_ref[at * RIM : (at + 1) * RIM, :] = ref[:RIM, SPLIT * DEPTH :]
    pack_head(q_ref, g_ref, HEADS - 1, lead_ref)


def pack_head(q_ref, g_ref, h, to_ref):
    rows = q_ref.shape[0] // PIECES
    for at, ref in enumerate((q_ref, g_ref)):
        for piece in range(PIECES):
            to_ref[2 * RIM :, cols(at * PIECES + piece)] = ref[piece * rows : (piece + 1) * rows, cols(h)]


def sent_of(ref, at):
    return jnp.concatenate([ref[2 * RIM :, cols(at * PIECES + piece)] for piece in range(PIECES)], axis=0)


def inside_pack_kernel(k_ref, v_ref, _, lead_ref):
    for at, ref in enumerate((k_ref, v_ref)):
        lead_ref[at] = ref[:RIM, :]


def own_kernel(count_ref, live_ref, lists_ref, q_ref, k_ref, v_ref, g_ref, table_ref, stats_ref, p_ref, prod_ref):
    tok = q_ref.shape[0]
    blocks = lists_ref.shape[0]
    count = count_ref[...]
    row = lax.broadcasted_iota(jnp.int32, (blocks, blocks), 0)
    lane = lax.broadcasted_iota(jnp.int32, (blocks, blocks), 1)
    live = jnp.sum(jnp.where(row == lane, live_ref[...], 0), axis=1, keepdims=True)
    odd = lax.axis_index("band") % 2
    slot = lax.broadcasted_iota(jnp.int32, (blocks, TABLE), 1)
    x_first = 8 + RB * odd
    i_first = 8 + RB * (1 - odd)
    ids = jnp.where(slot < 8, slot, jnp.where(slot < 8 + RB, slot - 8 + x_first, slot - 8 - RB + i_first))
    ids = jnp.where(slot < 8 + 2 * RB, ids, -1)
    table = table_of(lists_ref[...], live, ids, count, tok)
    table_ref[:TABLE] = table
    past = lax.broadcasted_iota(jnp.int32, (tok - RIM, tok), 0) + RIM >= count
    tail = [jnp.broadcast_to(table[at : at + 1], (BLK, tok)) for at in range(RB, tok // BLK)]
    table_ref[TABLE:] = jnp.where(past, NEG, jnp.concatenate(tail, axis=0))
    for h in range(HEADS):
        q, k, v, g = (ref[:, cols(h)] for ref in (q_ref, k_ref, v_ref, g_ref))
        top, p = own_exps(nt(k, q), table_ref)
        prod = nt(v, g)
        p_ref[h], prod_ref[h] = p, prod
        stats_ref[h] = rows_of(sums_of(top, p, prod))


def first_kernel(q_ref, g_ref, x_ref, table_ref, stats_ref, p_ref, prod_ref):
    for h in range(SPLIT):
        q, g = q_ref[:, cols(h)], g_ref[:, cols(h)]
        top, p = exps_of(nt(x_ref[:RIM, cols(h)], q), table_ref, 8)
        prod = nt(x_ref[RIM : 2 * RIM, cols(h)], g)
        p_ref[h], prod_ref[h] = p, prod
        stats_ref[h] = rows_of(sums_of(top, p, prod))


def rim_kernel(first, q_ref, g_ref, x_ref, i_ref, table_ref, stats_ref, *refs):
    gx_ref, final_ref, ds_ref, pi_ref, prodi_ref = refs[-5:]
    if not first:
        pack_head(q_ref, g_ref, HEADS - SENT, gx_ref)
    heads = range(x_ref.shape[1] // DEPTH)
    returned = len(heads) - (SENT if first else 0)
    parts = []
    for at in heads:
        h = first + at
        q, g = q_ref[:, cols(h)], g_ref[:, cols(h)]
        top, p = exps_of(nt(i_ref[0, :, cols(h)], q), table_ref, 8 + RB)
        prod = nt(i_ref[1, :, cols(h)], g)
        pi_ref[at], prodi_ref[at] = p, prod
        part_i = sums_of(top, p, prod)
        if first:
            top, p = exps_of(nt(x_ref[:RIM, cols(at)], q), table_ref, 8)
            prod = nt(x_ref[RIM : 2 * RIM, cols(at)], g)
            part_x = sums_of(top, p, prod)
        else:
            stats_x_ref, px_ref, prodx_ref = refs[:3]
            part_x, p, prod = known(stats_x_ref.at[h]), px_ref[h], prodx_ref[h]
        parts.append((part_i, part_x, p, prod))
    for at, (part_i, part_x, p, prod) in zip(heads, parts):
        h = first + at
        q, g = q_ref[:, cols(h)], g_ref[:, cols(h)]
        own = known(stats_ref.at[h])
        top, total, raw = merged(merged(own, part_i), part_x)
        inv = jnp.where(total > 0.0, 1.0 / jnp.where(total > 0.0, total, 1.0), 0.0)
        delta = raw * inv
        w, ds = grads_of(p, prod, jnp.exp2(part_x[0] - top) * inv, delta)
        if at < returned:
            gx_ref[:RIM, cols(at)] = nn(ds, q).astype(jnp.bfloat16)
            gx_ref[RIM : 2 * RIM, cols(at)] = nn(w, g).astype(jnp.bfloat16)
        else:
            rows = jnp.concatenate([table_ref[8 : 8 + RB] - top, inv, delta], axis=0)
            begin = 2 * RIM + (at - returned) * STATS
            gx_ref[begin : begin + STATS, : rows.shape[1]] = thirds_of(rows)
        ds_ref[at] = ds
        final_ref[at] = rows_of((jnp.exp2(own[0] - top) * inv, jnp.exp2(part_i[0] - top) * inv, delta))


def inside_kernel(q_ref, g_ref, *refs):
    gi_ref, ds_ref = refs[-2:]
    for h in range(HEADS):
        final_ref, pi_ref, prodi_ref = refs[:3] if h < SPLIT else refs[3:6]
        at = h if h < SPLIT else h - SPLIT
        q, g = q_ref[:, cols(h)], g_ref[:, cols(h)]
        w, ds = grads_of(pi_ref[at], prodi_ref[at], final_ref[at, 1:2], final_ref[at, 2:3])
        gi_ref[0, :, cols(h)] = nn(ds, q).astype(jnp.bfloat16)
        gi_ref[1, :, cols(h)] = nn(w, g).astype(jnp.bfloat16)
        ds_ref[h] = ds


def rest_kernel(q_ref, k_ref, v_ref, g_ref, p_ref, prod_ref, i_ref, dsi_ref, *refs):
    parts, (_, dq_ref, pk_ref, pv_ref, score_ref, products_ref) = (refs[:3], refs[3:6]), refs[6:]
    x_ref = parts[1][1]
    score_ref[...] = nt(k_ref[:RIM, cols(HEADS - 1)], sent_of(x_ref, 0))
    products_ref[...] = nt(v_ref[:RIM, cols(HEADS - 1)], sent_of(x_ref, 1))
    for h in range(HEADS):
        at = h if h < SPLIT else h - SPLIT
        final_ref, x_ref, dsx_ref = parts[0] if h < SPLIT else parts[1]
        q, k, g = (ref[:, cols(h)] for ref in (q_ref, k_ref, g_ref))
        w, ds = grads_of(p_ref[h], prod_ref[h], final_ref[at, 0:1], final_ref[at, 2:3])
        pk_ref[:, cols(h)] = nn(ds, q)
        pv_ref[:, cols(h)] = nn(w, g)
        frame_k = jnp.concatenate([k, x_ref[:RIM, cols(at)], i_ref[0, :, cols(h)]], axis=0)
        dq = tn(frame_k, jnp.concatenate([ds, dsx_ref[at], dsi_ref[h]], axis=0))
        dq_ref[:, cols(h)] = dq.T.astype(jnp.bfloat16)


def summed(own_ref, lead, gi_ref, slot, h):
    lead = own_ref[:RIM, cols(h)] + (lead + gi_ref[slot, :, cols(h)].astype(jnp.float32))
    return jnp.concatenate([lead, own_ref[RIM:, cols(h)]], axis=0).astype(jnp.bfloat16)


def done_kernel(
    k_ref, v_ref, dq_in, pk_ref, pv_ref, gx_ref, gi_ref, dq_ref, dk_ref, dv_ref, score_ref, products_ref, dk_buf, dv_buf, sems
):
    span = pl.ds(0, dk_buf.shape[1])
    copies = [
        pltpu.make_async_copy(dq_in, dq_ref, sems.at[0]),
        pltpu.make_async_copy(dk_buf, dk_ref.at[:, span], sems.at[1]),
        pltpu.make_async_copy(dv_buf, dv_ref.at[:, span], sems.at[2]),
    ]
    copies[0].start()
    for slot, (own, buf) in enumerate(((pk_ref, dk_buf), (pv_ref, dv_buf))):
        for h in range(SPLIT):
            lead = gx_ref[slot * RIM : (slot + 1) * RIM, cols(h)].astype(jnp.float32)
            buf[:, cols(h)] = summed(own, lead, gi_ref, slot, h)
        copies[1 + slot].start()
    score_ref[...] = nt(k_ref[:RIM, cols(HEADS - SENT)], sent_of(gx_ref, 0))
    products_ref[...] = nt(v_ref[:RIM, cols(HEADS - SENT)], sent_of(gx_ref, 1))
    for copy in copies:
        copy.wait()


def add_kernel(pk_ref, pv_ref, gx_ref, gi_ref, *refs):
    sent, (_, _, dk_ref, dv_ref, dk_buf, dv_buf, sems) = (refs[:3], refs[3:6]), refs[6:]
    heads = HEADS - SPLIT
    returned = heads - SENT
    leads = {}
    for n, (from_ref, score_ref, prod_ref) in enumerate(sent):
        begin = 2 * RIM + n * STATS
        rows = whole_of(gx_ref[begin : begin + STATS, : score_ref.shape[1]].astype(jnp.float32))
        blocks = [jnp.exp2(score_ref[e * BLK : (e + 1) * BLK] * SCALE + rows[e : e + 1]) for e in range(RB)]
        w, ds = grads_of(jnp.concatenate(blocks, axis=0), prod_ref[...], rows[RB : RB + 1], rows[RB + 1 : RB + 2])
        leads[returned + n] = nn(ds, sent_of(from_ref, 0)), nn(w, sent_of(from_ref, 1))
    span = pl.ds(SPLIT * DEPTH, heads * DEPTH)
    copies = [
        pltpu.make_async_copy(buf, out.at[:, span], sems.at[slot])
        for slot, (buf, out) in enumerate(((dk_buf, dk_ref), (dv_buf, dv_ref)))
    ]
    for slot, (own, buf) in enumerate(((pk_ref, dk_buf), (pv_ref, dv_buf))):
        for at in range(heads):
            if at in leads:
                lead = leads[at][slot]
            else:
                lead = gx_ref[slot * RIM : (slot + 1) * RIM, cols(at)].astype(jnp.float32)
            buf[:, cols(at)] = summed(own, lead, gi_ref, slot, SPLIT + at)
        copies[slot].start()
    for copy in copies:
        copy.wait()


VMEM = pl.BlockSpec(memory_space=pltpu.VMEM)
HBM = pl.BlockSpec(memory_space=pltpu.HBM)
ANY = pl.BlockSpec(memory_space=pl.ANY)


def call(body, name, ins, outs, out_specs, args, scratch=(), alias=None, limit=24):
    return pl.pallas_call(
        body,
        in_specs=ins,
        out_specs=out_specs,
        out_shape=outs,
        scratch_shapes=scratch,
        input_output_aliases=alias or {},
        compiler_params=pltpu.CompilerParams(vmem_limit_bytes=int(limit * MIB)),
        cost_estimate=pl.CostEstimate(flops=WEIGHT[name] * MEGA, bytes_accessed=1000, transcendentals=0),
        name=name,
    )(*args)


def shape(*dims, dtype=jnp.bfloat16):
    return jax.ShapeDtypeStruct(dims, dtype)


def on_device(queries, keys, values, out_grad, band_counts, block_lists, slot_counts):
    tok, width = queries.shape
    f32 = functools.partial(shape, dtype=jnp.float32)
    cuts = ((0, SPLIT), (SPLIT, HEADS))
    part = HEADS - SPLIT
    q, k, v, g = queries, keys, values, out_grad
    lead_a = call(
        load_kernel,
        "load_bands",
        [HBM] * 2,
        shape(2 * RIM, SPLIT * DEPTH),
        VMEM,
        (k, v),
        [pltpu.SemaphoreType.DMA((2,))],
        limit=LOAD_LIMIT,
    )
    lead_b = call(pack_kernel, "pack_leads", [VMEM] * 4, shape(2 * RIM + tok // PIECES, part * DEPTH), VMEM, (k, v, q, g))
    x_a, x_b = swap_across(lead_a), swap_across(lead_b)
    lead_i = call(inside_pack_kernel, "pack_inside", [VMEM] * 2 + [ANY], shape(2, RIM, width), VMEM, (k, v, lead_b))
    i = swap_inside(lead_i)
    table, stats, p, prod = call(
        own_kernel,
        "own_stats",
        [VMEM] * 7,
        [f32(TABLE + tok - RIM, tok), f32(HEADS, 8, tok), f32(HEADS, tok, tok), f32(HEADS, tok, tok)],
        [VMEM] * 4,
        (band_counts[:, None], slot_counts[None], block_lists, q, k, v, g),
    )
    stats_x, px, prodx = call(
        first_kernel,
        "first_stats",
        [VMEM] * 4,
        [f32(SPLIT, 8, tok), f32(SPLIT, RIM, tok), f32(SPLIT, RIM, tok)],
        [VMEM] * 3,
        (q, g, x_a, table),
    )

    def rim(first, x, *more):
        heads = x.shape[1] // DEPTH
        gx = (2 * RIM + SENT * STATS, (heads - SENT) * DEPTH) if first else (x.shape[0] + tok // PIECES, x.shape[1])
        return call(
            functools.partial(rim_kernel, first),
            "rim_grads",
            [VMEM] * (6 + len(more)),
            [shape(*gx), f32(heads, 8, tok), shape(heads, RIM, tok), f32(heads, RIM, tok), f32(heads, RIM, tok)],
            [VMEM] * 5,
            (q, g, x, i, table, stats) + more,
        )

    gx_a, final_a, dsx_a, *inside_a = rim(0, x_a, stats_x, px, prodx)
    gx_a = swap_across(gx_a)
    gx_b, final_b, dsx_b, *inside_b = rim(SPLIT, x_b)
    gx_b = swap_across(gx_b)
    gi, ds_i = call(
        inside_kernel,
        "inside_grads",
        [VMEM] * 8,
        [shape(2, RIM, width), shape(HEADS, RIM, tok)],
        [VMEM] * 2,
        (q, g, final_a, *inside_a, final_b, *inside_b),
    )
    gi = swap_inside(gi)

    dq, pk, pv, *last = call(
        rest_kernel,
        "rest_grads",
        [VMEM] * 14 + [ANY],
        [shape(tok, width), f32(tok, width), f32(tok, width), f32(RIM, tok), f32(RIM, tok)],
        [VMEM] * 5,
        (q, k, v, g, p, prod, i, ds_i, final_a, x_a, dsx_a, final_b, x_b, dsx_b, gx_a),
    )
    dq, dk, dv, *other = call(
        done_kernel,
        "done_grads",
        [VMEM] * 7,
        [shape(tok, width)] * 3 + [f32(RIM, tok)] * 2,
        [ANY] * 3 + [VMEM] * 2,
        (k, v, dq, pk, pv, gx_a, gi),
        [pltpu.VMEM((tok, SPLIT * DEPTH), jnp.bfloat16)] * 2 + [pltpu.SemaphoreType.DMA((3,))],
    )
    dk, dv = call(
        add_kernel,
        "add_rims",
        [VMEM] * 10 + [ANY] * 2,
        [shape(tok, width)] * 2,
        [ANY] * 2,
        (pk, pv, gx_b, gi, gx_a, *other, x_b, *last, dk, dv),
        [pltpu.VMEM((tok, part * DEPTH), jnp.bfloat16)] * 2 + [pltpu.SemaphoreType.DMA((2,))],
        {10: 0, 11: 1},
    )
    return dq, dk, dv


def solution(mesh):
    placed = P(("member", "band"), None)
    flat = P(("member", "band"))
    return jax.shard_map(
        on_device,
        mesh=mesh,
        in_specs=(placed, placed, placed, placed, flat, placed, flat),
        out_specs=(placed, placed, placed),
        check_vma=False,
    )
```

```python
import functools
import jax
import jax.numpy as jnp
from jax import lax
from jax.experimental import pallas as pl
from jax.experimental.pallas import tpu as pltpu
from jax.sharding import PartitionSpec as P

HEADS = 8
DEPTH = 128
BLK = 32
RB = 6
RIM = RB * BLK
TABLE = 32
LOG2E = 1.4426950408889634
NEG = -1e30
FLOOR = -1e20
MIB = 1024 * 1024
LOAD_LIMIT = 53.5
SPLIT = 4
SENT = 2
PIECES = 2
STATS = 32
MEGA = 10**6
WEIGHT = {
    "load_bands": 5500,
    "pack_leads": 1,
    "pack_inside": 1,
    "own_stats": 1,
    "first_stats": 11000,
    "rim_grads": 1,
    "inside_grads": 1,
    "rest_grads": 11000,
    "done_grads": 11000,
    "final_sums": 1,
}


def nt(a, b):
    return lax.dot_general(a, b, (((1,), (1,)), ((), ())), preferred_element_type=jnp.float32)


def tn(a, b):
    return lax.dot_general(a, b, (((0,), (0,)), ((), ())), preferred_element_type=jnp.float32)


def nn(a, b):
    return jnp.dot(a, b, preferred_element_type=jnp.float32)


def cols(h):
    return slice(h * DEPTH, (h + 1) * DEPTH)


SCALE = DEPTH ** -0.5 * LOG2E


def exps_of(score, bias, first):
    parts = [score[at * BLK : (at + 1) * BLK] for at in range(score.shape[0] // BLK)]
    rows = [bias[first + at : first + at + 1, :] for at in range(len(parts))]
    tops = [jnp.max(part, axis=0, keepdims=True) * SCALE + row for part, row in zip(parts, rows)]
    top = functools.reduce(jnp.maximum, tops, jnp.full_like(tops[0], FLOOR))
    return top, jnp.concatenate([jnp.exp2(part * SCALE + (row - top)) for part, row in zip(parts, rows)], axis=0)


def own_exps(score, bias):
    lead, tail = score[:RIM], score[RIM:] * SCALE + bias[TABLE:, :]
    parts = [lead[at * BLK : (at + 1) * BLK] for at in range(RB)]
    rows = [bias[at : at + 1, :] for at in range(RB)]
    tops = [jnp.max(part, axis=0, keepdims=True) * SCALE + row for part, row in zip(parts, rows)]
    top = functools.reduce(jnp.maximum, tops, jnp.maximum(jnp.max(tail, axis=0, keepdims=True), FLOOR))
    exps = [jnp.exp2(part * SCALE + (row - top)) for part, row in zip(parts, rows)]
    return top, jnp.concatenate(exps + [jnp.exp2(tail - top)], axis=0)


def table_of(lists, live, ids, count, tok):
    blocks, slots = lists.shape
    hit = jnp.zeros((blocks, ids.shape[1]), jnp.float32)
    for l in range(slots):
        hit = jnp.where((lists[:, l : l + 1] == ids) & (live > l), 1.0, hit)
    lane = lax.broadcasted_iota(jnp.int32, (blocks, tok), 1)
    row = lax.broadcasted_iota(jnp.int32, (blocks, tok), 0)
    spread = jnp.where((lane // BLK == row) & (lane < count), 1.0, 0.0)
    return jnp.where(tn(hit, spread) > 0.5, 0.0, NEG)


def merged(a, b):
    top = jnp.maximum(a[0], b[0])
    fa, fb = jnp.exp2(a[0] - top), jnp.exp2(b[0] - top)
    return top, a[1] * fa + b[1] * fb, a[2] * fa + b[2] * fb


def sums_of(top, p, prod):
    return top, jnp.sum(p, axis=0, keepdims=True), jnp.sum(p * prod, axis=0, keepdims=True)


def rows_of(values):
    pad = jnp.zeros((8 - len(values), values[0].shape[1]), jnp.float32)
    return jnp.concatenate(tuple(values) + (pad,), axis=0)


def known(ref):
    return ref[0:1], ref[1:2], ref[2:3]


def thirds_of(rows):
    high = rows.astype(jnp.bfloat16)
    left = rows - high.astype(jnp.float32)
    middle = left.astype(jnp.bfloat16)
    low = (left - middle.astype(jnp.float32)).astype(jnp.bfloat16)
    parts = [part.astype(jnp.float32) for part in (high, middle, low)]
    return jnp.concatenate(parts + [jnp.zeros_like(rows)], axis=0).astype(jnp.bfloat16)


def whole_of(parts):
    high, middle, low = (parts[at * 8 : (at + 1) * 8] for at in range(3))
    return high + (middle + low)


def grads_of(p, prod, factor, delta):
    w = (p * factor).astype(jnp.bfloat16)
    ds = (p * (factor * (DEPTH ** -0.5)) * (prod - delta)).astype(jnp.bfloat16)
    return w, ds


def swap_across(x):
    count = lax.axis_size("band")
    pairs = [(at, at + 1) for at in range(1, count - 1, 2)]
    return lax.ppermute(x, "band", pairs + [(b, a) for a, b in pairs])


def swap_inside(x):
    return lax.ppermute(x, "band", [(at, at ^ 1) for at in range(lax.axis_size("band"))])


def load_kernel(k_ref, v_ref, lead_ref, sems):
    copies = [
        pltpu.make_async_copy(
            src.at[pl.ds(0, RIM), pl.ds(0, SPLIT * DEPTH)], lead_ref.at[pl.ds(at * RIM, RIM), :], sems.at[at]
        )
        for at, src in enumerate((k_ref, v_ref))
    ]
    for copy in copies:
        copy.start()
    for copy in copies:
        copy.wait()


def pack_kernel(k_ref, v_ref, q_ref, g_ref, lead_ref):
    for at, ref in enumerate((k_ref, v_ref)):
        lead_ref[at * RIM : (at + 1) * RIM, :] = ref[:RIM, SPLIT * DEPTH :]
    pack_head(q_ref, g_ref, HEADS - 1, lead_ref)


def pack_head(q_ref, g_ref, h, to_ref):
    rows = q_ref.shape[0] // PIECES
    for at, ref in enumerate((q_ref, g_ref)):
        for piece in range(PIECES):
            to_ref[2 * RIM :, cols(at * PIECES + piece)] = ref[piece * rows : (piece + 1) * rows, cols(h)]


def sent_of(ref, at):
    return jnp.concatenate([ref[2 * RIM :, cols(at * PIECES + piece)] for piece in range(PIECES)], axis=0)


def inside_pack_kernel(k_ref, v_ref, _, lead_ref):
    for at, ref in enumerate((k_ref, v_ref)):
        lead_ref[at] = ref[:RIM, :]


def own_kernel(count_ref, live_ref, lists_ref, q_ref, k_ref, v_ref, g_ref, table_ref, stats_ref, p_ref, prod_ref):
    tok = q_ref.shape[0]
    blocks = lists_ref.shape[0]
    count = count_ref[...]
    row = lax.broadcasted_iota(jnp.int32, (blocks, blocks), 0)
    lane = lax.broadcasted_iota(jnp.int32, (blocks, blocks), 1)
    live = jnp.sum(jnp.where(row == lane, live_ref[...], 0), axis=1, keepdims=True)
    odd = lax.axis_index("band") % 2
    slot = lax.broadcasted_iota(jnp.int32, (blocks, TABLE), 1)
    x_first = 8 + RB * odd
    i_first = 8 + RB * (1 - odd)
    ids = jnp.where(slot < 8, slot, jnp.where(slot < 8 + RB, slot - 8 + x_first, slot - 8 - RB + i_first))
    ids = jnp.where(slot < 8 + 2 * RB, ids, -1)
    table = table_of(lists_ref[...], live, ids, count, tok)
    table_ref[:TABLE] = table
    past = lax.broadcasted_iota(jnp.int32, (tok - RIM, tok), 0) + RIM >= count
    tail = [jnp.broadcast_to(table[at : at + 1], (BLK, tok)) for at in range(RB, tok // BLK)]
    table_ref[TABLE:] = jnp.where(past, NEG, jnp.concatenate(tail, axis=0))
    for h in range(HEADS):
        q, k, v, g = (ref[:, cols(h)] for ref in (q_ref, k_ref, v_ref, g_ref))
        top, p = own_exps(nt(k, q), table_ref)
        prod = nt(v, g)
        p_ref[h], prod_ref[h] = p, prod
        stats_ref[h] = rows_of(sums_of(top, p, prod))


def first_kernel(q_ref, g_ref, x_ref, table_ref, stats_ref, p_ref, prod_ref):
    for h in range(SPLIT):
        q, g = q_ref[:, cols(h)], g_ref[:, cols(h)]
        top, p = exps_of(nt(x_ref[:RIM, cols(h)], q), table_ref, 8)
        prod = nt(x_ref[RIM : 2 * RIM, cols(h)], g)
        p_ref[h], prod_ref[h] = p, prod
        stats_ref[h] = rows_of(sums_of(top, p, prod))


def rim_kernel(first, q_ref, g_ref, x_ref, i_ref, table_ref, stats_ref, *refs):
    gx_ref, final_ref, ds_ref, pi_ref, prodi_ref = refs[-5:]
    if not first:
        pack_head(q_ref, g_ref, HEADS - SENT, gx_ref)
    heads = range(x_ref.shape[1] // DEPTH)
    returned = len(heads) - (SENT if first else 0)
    parts = []
    for at in heads:
        h = first + at
        q, g = q_ref[:, cols(h)], g_ref[:, cols(h)]
        top, p = exps_of(nt(i_ref[0, :, cols(h)], q), table_ref, 8 + RB)
        prod = nt(i_ref[1, :, cols(h)], g)
        pi_ref[at], prodi_ref[at] = p, prod
        part_i = sums_of(top, p, prod)
        if first:
            top, p = exps_of(nt(x_ref[:RIM, cols(at)], q), table_ref, 8)
            prod = nt(x_ref[RIM : 2 * RIM, cols(at)], g)
            part_x = sums_of(top, p, prod)
        else:
            stats_x_ref, px_ref, prodx_ref = refs[:3]
            part_x, p, prod = known(stats_x_ref.at[h]), px_ref[h], prodx_ref[h]
        parts.append((part_i, part_x, p, prod))
    for at, (part_i, part_x, p, prod) in zip(heads, parts):
        h = first + at
        q, g = q_ref[:, cols(h)], g_ref[:, cols(h)]
        own = known(stats_ref.at[h])
        top, total, raw = merged(merged(own, part_i), part_x)
        inv = jnp.where(total > 0.0, 1.0 / jnp.where(total > 0.0, total, 1.0), 0.0)
        delta = raw * inv
        w, ds = grads_of(p, prod, jnp.exp2(part_x[0] - top) * inv, delta)
        if at < returned:
            gx_ref[:RIM, cols(at)] = nn(ds, q).astype(jnp.bfloat16)
            gx_ref[RIM : 2 * RIM, cols(at)] = nn(w, g).astype(jnp.bfloat16)
        else:
            rows = jnp.concatenate([table_ref[8 : 8 + RB] - top, inv, delta], axis=0)
            begin = 2 * RIM + (at - returned) * STATS
            gx_ref[begin : begin + STATS, : rows.shape[1]] = thirds_of(rows)
        ds_ref[at] = ds
        final_ref[at] = rows_of((jnp.exp2(own[0] - top) * inv, jnp.exp2(part_i[0] - top) * inv, delta))


def inside_kernel(q_ref, g_ref, *refs):
    gi_ref, ds_ref = refs[-2:]
    for h in range(HEADS):
        final_ref, pi_ref, prodi_ref = refs[:3] if h < SPLIT else refs[3:6]
        at = h if h < SPLIT else h - SPLIT
        q, g = q_ref[:, cols(h)], g_ref[:, cols(h)]
        w, ds = grads_of(pi_ref[at], prodi_ref[at], final_ref[at, 1:2], final_ref[at, 2:3])
        gi_ref[0, :, cols(h)] = nn(ds, q).astype(jnp.bfloat16)
        gi_ref[1, :, cols(h)] = nn(w, g).astype(jnp.bfloat16)
        ds_ref[h] = ds


def rest_kernel(q_ref, k_ref, v_ref, g_ref, p_ref, prod_ref, i_ref, dsi_ref, *refs):
    parts, (_, dq_ref, pk_ref, pv_ref, score_ref, products_ref, dq_buf, sems) = (refs[:3], refs[3:6]), refs[6:]
    x_ref = parts[1][1]
    score_ref[...] = nt(k_ref[:RIM, cols(HEADS - 1)], sent_of(x_ref, 0))
    products_ref[...] = nt(v_ref[:RIM, cols(HEADS - 1)], sent_of(x_ref, 1))
    copies = []
    for h in range(HEADS):
        at = h if h < SPLIT else h - SPLIT
        final_ref, x_ref, dsx_ref = parts[0] if h < SPLIT else parts[1]
        q, k, g = (ref[:, cols(h)] for ref in (q_ref, k_ref, g_ref))
        w, ds = grads_of(p_ref[h], prod_ref[h], final_ref[at, 0:1], final_ref[at, 2:3])
        pk_ref[:, cols(h)] = nn(ds, q)
        pv_ref[:, cols(h)] = nn(w, g)
        frame_k = jnp.concatenate([k, x_ref[:RIM, cols(at)], i_ref[0, :, cols(h)]], axis=0)
        dq = tn(frame_k, jnp.concatenate([ds, dsx_ref[at], dsi_ref[h]], axis=0))
        dq_buf[:, cols(h)] = dq.T.astype(jnp.bfloat16)
        if at == SPLIT - 1:
            span = (slice(None), pl.ds((h + 1 - SPLIT) * DEPTH, SPLIT * DEPTH))
            copies.append(pltpu.make_async_copy(dq_buf.at[span], dq_ref.at[span], sems.at[len(copies)]))
            copies[-1].start()
    for copy in copies:
        copy.wait()


def summed(own_ref, lead, gi_ref, slot, h):
    lead = own_ref[:RIM, cols(h)] + (lead + gi_ref[slot, :, cols(h)].astype(jnp.float32))
    return jnp.concatenate([lead, own_ref[RIM:, cols(h)]], axis=0).astype(jnp.bfloat16)


def done_kernel(k_ref, v_ref, pk_ref, pv_ref, gx_ref, gi_ref, dk_ref, dv_ref, score_ref, products_ref):
    for slot, (own, out) in enumerate(((pk_ref, dk_ref), (pv_ref, dv_ref))):
        for h in range(SPLIT):
            lead = gx_ref[slot * RIM : (slot + 1) * RIM, cols(h)].astype(jnp.float32)
            out[:, cols(h)] = summed(own, lead, gi_ref, slot, h)
    score_ref[...] = nt(k_ref[:RIM, cols(HEADS - SENT)], sent_of(gx_ref, 0))
    products_ref[...] = nt(v_ref[:RIM, cols(HEADS - SENT)], sent_of(gx_ref, 1))


def final_kernel(dk_in, dv_in, pk_ref, pv_ref, gx_ref, gi_ref, *refs):
    sent, (dk_ref, dv_ref, dk_buf, dv_buf, sems) = (refs[:3], refs[3:6]), refs[6:]
    heads = HEADS - SPLIT
    early = pl.ds(0, SPLIT * DEPTH)
    late = pl.ds(SPLIT * DEPTH, heads * DEPTH)
    copies = [
        pltpu.make_async_copy(dk_in, dk_ref.at[:, early], sems.at[0]),
        pltpu.make_async_copy(dv_in, dv_ref.at[:, early], sems.at[1]),
        pltpu.make_async_copy(dk_buf, dk_ref.at[:, late], sems.at[2]),
        pltpu.make_async_copy(dv_buf, dv_ref.at[:, late], sems.at[3]),
    ]
    for copy in copies[:2]:
        copy.start()
    returned = heads - SENT
    leads = {}
    for n, (from_ref, score_ref, prod_ref) in enumerate(sent):
        begin = 2 * RIM + n * STATS
        rows = whole_of(gx_ref[begin : begin + STATS, : score_ref.shape[1]].astype(jnp.float32))
        blocks = [jnp.exp2(score_ref[e * BLK : (e + 1) * BLK] * SCALE + rows[e : e + 1]) for e in range(RB)]
        w, ds = grads_of(jnp.concatenate(blocks, axis=0), prod_ref[...], rows[RB : RB + 1], rows[RB + 1 : RB + 2])
        leads[returned + n] = nn(ds, sent_of(from_ref, 0)), nn(w, sent_of(from_ref, 1))
    for slot, (own, buf) in enumerate(((pk_ref, dk_buf), (pv_ref, dv_buf))):
        for at in range(heads):
            if at in leads:
                lead = leads[at][slot]
            else:
                lead = gx_ref[slot * RIM : (slot + 1) * RIM, cols(at)].astype(jnp.float32)
            buf[:, cols(at)] = summed(own, lead, gi_ref, slot, SPLIT + at)
        copies[2 + slot].start()
    for copy in copies:
        copy.wait()


VMEM = pl.BlockSpec(memory_space=pltpu.VMEM)
HBM = pl.BlockSpec(memory_space=pltpu.HBM)
ANY = pl.BlockSpec(memory_space=pl.ANY)


def call(body, name, ins, outs, out_specs, args, scratch=(), alias=None, limit=24):
    return pl.pallas_call(
        body,
        in_specs=ins,
        out_specs=out_specs,
        out_shape=outs,
        scratch_shapes=scratch,
        input_output_aliases=alias or {},
        compiler_params=pltpu.CompilerParams(vmem_limit_bytes=int(limit * MIB)),
        cost_estimate=pl.CostEstimate(flops=WEIGHT[name] * MEGA, bytes_accessed=1000, transcendentals=0),
        name=name,
    )(*args)


def shape(*dims, dtype=jnp.bfloat16):
    return jax.ShapeDtypeStruct(dims, dtype)


def on_device(queries, keys, values, out_grad, band_counts, block_lists, slot_counts):
    tok, width = queries.shape
    f32 = functools.partial(shape, dtype=jnp.float32)
    cuts = ((0, SPLIT), (SPLIT, HEADS))
    part = HEADS - SPLIT
    q, k, v, g = queries, keys, values, out_grad
    lead_a = call(
        load_kernel,
        "load_bands",
        [HBM] * 2,
        shape(2 * RIM, SPLIT * DEPTH),
        VMEM,
        (k, v),
        [pltpu.SemaphoreType.DMA((2,))],
        limit=LOAD_LIMIT,
    )
    lead_b = call(pack_kernel, "pack_leads", [VMEM] * 4, shape(2 * RIM + tok // PIECES, part * DEPTH), VMEM, (k, v, q, g))
    x_a, x_b = swap_across(lead_a), swap_across(lead_b)
    lead_i = call(inside_pack_kernel, "pack_inside", [VMEM] * 2 + [ANY], shape(2, RIM, width), VMEM, (k, v, lead_b))
    i = swap_inside(lead_i)
    table, stats, p, prod = call(
        own_kernel,
        "own_stats",
        [VMEM] * 7,
        [f32(TABLE + tok - RIM, tok), f32(HEADS, 8, tok), f32(HEADS, tok, tok), f32(HEADS, tok, tok)],
        [VMEM] * 4,
        (band_counts[:, None], slot_counts[None], block_lists, q, k, v, g),
    )
    stats_x, px, prodx = call(
        first_kernel,
        "first_stats",
        [VMEM] * 4,
        [f32(SPLIT, 8, tok), f32(SPLIT, RIM, tok), f32(SPLIT, RIM, tok)],
        [VMEM] * 3,
        (q, g, x_a, table),
    )

    def rim(first, x, *more):
        heads = x.shape[1] // DEPTH
        gx = (2 * RIM + SENT * STATS, (heads - SENT) * DEPTH) if first else (x.shape[0] + tok // PIECES, x.shape[1])
        return call(
            functools.partial(rim_kernel, first),
            "rim_grads",
            [VMEM] * (6 + len(more)),
            [shape(*gx), f32(heads, 8, tok), shape(heads, RIM, tok), f32(heads, RIM, tok), f32(heads, RIM, tok)],
            [VMEM] * 5,
            (q, g, x, i, table, stats) + more,
        )

    gx_a, final_a, dsx_a, *inside_a = rim(0, x_a, stats_x, px, prodx)
    gx_a = swap_across(gx_a)
    gx_b, final_b, dsx_b, *inside_b = rim(SPLIT, x_b)
    gx_b = swap_across(gx_b)
    gi, ds_i = call(
        inside_kernel,
        "inside_grads",
        [VMEM] * 8,
        [shape(2, RIM, width), shape(HEADS, RIM, tok)],
        [VMEM] * 2,
        (q, g, final_a, *inside_a, final_b, *inside_b),
    )
    gi = swap_inside(gi)

    dq, pk, pv, *last = call(
        rest_kernel,
        "rest_grads",
        [VMEM] * 14 + [ANY],
        [shape(tok, width), f32(tok, width), f32(tok, width), f32(RIM, tok), f32(RIM, tok)],
        [ANY] + [VMEM] * 4,
        (q, k, v, g, p, prod, i, ds_i, final_a, x_a, dsx_a, final_b, x_b, dsx_b, gx_a),
        [pltpu.VMEM((tok, width), jnp.bfloat16), pltpu.SemaphoreType.DMA((2,))],
    )
    dk_a, dv_a, *other = call(
        done_kernel,
        "done_grads",
        [VMEM] * 6,
        [shape(tok, SPLIT * DEPTH)] * 2 + [f32(RIM, tok)] * 2,
        [VMEM] * 4,
        (k, v, pk, pv, gx_a, gi),
    )
    dk, dv = call(
        final_kernel,
        "final_sums",
        [VMEM] * 12,
        [shape(tok, width)] * 2,
        [ANY] * 2,
        (dk_a, dv_a, pk, pv, gx_b, gi, gx_a, *other, x_b, *last),
        [pltpu.VMEM((tok, part * DEPTH), jnp.bfloat16)] * 2 + [pltpu.SemaphoreType.DMA((4,))],
    )
    return dq, dk, dv


def solution(mesh):
    placed = P(("member", "band"), None)
    flat = P(("member", "band"))
    return jax.shard_map(
        on_device,
        mesh=mesh,
        in_specs=(placed, placed, placed, placed, flat, placed, flat),
        out_specs=(placed, placed, placed),
        check_vma=False,
    )
```

```python
import functools
import jax
import jax.numpy as jnp
from jax import lax
from jax.experimental import pallas as pl
from jax.experimental.pallas import tpu as pltpu
from jax.sharding import PartitionSpec as P

HEADS = 8
DEPTH = 128
BLK = 32
RB = 6
RIM = RB * BLK
TABLE = 32
LOG2E = 1.4426950408889634
NEG = -1e30
FLOOR = -1e20
MIB = 1024 * 1024
LOAD_LIMIT = 53.5
SPLIT = 4
SENT = 2
PIECES = 2
STATS = 32
MEGA = 10**6
WEIGHT = {
    "load_bands": 5500,
    "pack_leads": 1,
    "pack_inside": 1,
    "own_stats": 1,
    "first_stats": 11000,
    "rim_grads": 1,
    "inside_grads": 1,
    "rest_grads": 11000,
    "done_grads": 11000,
    "final_sums": 1,
}


def nt(a, b):
    return lax.dot_general(a, b, (((1,), (1,)), ((), ())), preferred_element_type=jnp.float32)


def tn(a, b):
    return lax.dot_general(a, b, (((0,), (0,)), ((), ())), preferred_element_type=jnp.float32)


def nn(a, b):
    return jnp.dot(a, b, preferred_element_type=jnp.float32)


def cols(h):
    return slice(h * DEPTH, (h + 1) * DEPTH)


SCALE = DEPTH ** -0.5 * LOG2E


def exps_of(score, bias, first):
    parts = [score[at * BLK : (at + 1) * BLK] for at in range(score.shape[0] // BLK)]
    rows = [bias[first + at : first + at + 1, :] for at in range(len(parts))]
    tops = [jnp.max(part, axis=0, keepdims=True) * SCALE + row for part, row in zip(parts, rows)]
    top = functools.reduce(jnp.maximum, tops, jnp.full_like(tops[0], FLOOR))
    return top, jnp.concatenate([jnp.exp2(part * SCALE + (row - top)) for part, row in zip(parts, rows)], axis=0)


def own_exps(score, bias):
    lead, tail = score[:RIM], score[RIM:] * SCALE + bias[TABLE:, :]
    parts = [lead[at * BLK : (at + 1) * BLK] for at in range(RB)]
    rows = [bias[at : at + 1, :] for at in range(RB)]
    tops = [jnp.max(part, axis=0, keepdims=True) * SCALE + row for part, row in zip(parts, rows)]
    top = functools.reduce(jnp.maximum, tops, jnp.maximum(jnp.max(tail, axis=0, keepdims=True), FLOOR))
    exps = [jnp.exp2(part * SCALE + (row - top)) for part, row in zip(parts, rows)]
    return top, jnp.concatenate(exps + [jnp.exp2(tail - top)], axis=0)


def table_of(lists, live, ids, count, tok):
    blocks, slots = lists.shape
    hit = jnp.zeros((blocks, ids.shape[1]), jnp.float32)
    for l in range(slots):
        hit = jnp.where((lists[:, l : l + 1] == ids) & (live > l), 1.0, hit)
    lane = lax.broadcasted_iota(jnp.int32, (blocks, tok), 1)
    row = lax.broadcasted_iota(jnp.int32, (blocks, tok), 0)
    spread = jnp.where((lane // BLK == row) & (lane < count), 1.0, 0.0)
    return jnp.where(tn(hit, spread) > 0.5, 0.0, NEG)


def merged(a, b):
    top = jnp.maximum(a[0], b[0])
    fa, fb = jnp.exp2(a[0] - top), jnp.exp2(b[0] - top)
    return top, a[1] * fa + b[1] * fb, a[2] * fa + b[2] * fb


def sums_of(top, p, prod):
    return top, jnp.sum(p, axis=0, keepdims=True), jnp.sum(p * prod, axis=0, keepdims=True)


def rows_of(values):
    pad = jnp.zeros((8 - len(values), values[0].shape[1]), jnp.float32)
    return jnp.concatenate(tuple(values) + (pad,), axis=0)


def known(ref):
    return ref[0:1], ref[1:2], ref[2:3]


def thirds_of(rows):
    high = rows.astype(jnp.bfloat16)
    left = rows - high.astype(jnp.float32)
    middle = left.astype(jnp.bfloat16)
    low = (left - middle.astype(jnp.float32)).astype(jnp.bfloat16)
    parts = [part.astype(jnp.float32) for part in (high, middle, low)]
    return jnp.concatenate(parts + [jnp.zeros_like(rows)], axis=0).astype(jnp.bfloat16)


def whole_of(parts):
    high, middle, low = (parts[at * 8 : (at + 1) * 8] for at in range(3))
    return high + (middle + low)


def grads_of(p, prod, factor, delta):
    w = (p * factor).astype(jnp.bfloat16)
    ds = (p * (factor * (DEPTH ** -0.5)) * (prod - delta)).astype(jnp.bfloat16)
    return w, ds


def swap_across(x):
    count = lax.axis_size("band")
    pairs = [(at, at + 1) for at in range(1, count - 1, 2)]
    return lax.ppermute(x, "band", pairs + [(b, a) for a, b in pairs])


def swap_inside(x):
    return lax.ppermute(x, "band", [(at, at ^ 1) for at in range(lax.axis_size("band"))])


def load_kernel(k_ref, v_ref, lead_ref, sems):
    copies = [
        pltpu.make_async_copy(
            src.at[pl.ds(0, RIM), pl.ds(0, SPLIT * DEPTH)], lead_ref.at[pl.ds(at * RIM, RIM), :], sems.at[at]
        )
        for at, src in enumerate((k_ref, v_ref))
    ]
    for copy in copies:
        copy.start()
    for copy in copies:
        copy.wait()


def pack_kernel(k_ref, v_ref, q_ref, g_ref, lead_ref):
    for at, ref in enumerate((k_ref, v_ref)):
        lead_ref[at * RIM : (at + 1) * RIM, :] = ref[:RIM, SPLIT * DEPTH :]
    pack_head(q_ref, g_ref, HEADS - 1, lead_ref)


def pack_head(q_ref, g_ref, h, to_ref):
    rows = q_ref.shape[0] // PIECES
    for at, ref in enumerate((q_ref, g_ref)):
        for piece in range(PIECES):
            to_ref[2 * RIM :, cols(at * PIECES + piece)] = ref[piece * rows : (piece + 1) * rows, cols(h)]


def sent_of(ref, at):
    return jnp.concatenate([ref[2 * RIM :, cols(at * PIECES + piece)] for piece in range(PIECES)], axis=0)


def inside_pack_kernel(k_ref, v_ref, _, lead_ref):
    for at, ref in enumerate((k_ref, v_ref)):
        lead_ref[at] = ref[:RIM, :]


def own_kernel(count_ref, live_ref, lists_ref, q_ref, k_ref, v_ref, g_ref, table_ref, stats_ref, p_ref, prod_ref):
    tok = q_ref.shape[0]
    blocks = lists_ref.shape[0]
    count = count_ref[...]
    row = lax.broadcasted_iota(jnp.int32, (blocks, blocks), 0)
    lane = lax.broadcasted_iota(jnp.int32, (blocks, blocks), 1)
    live = jnp.sum(jnp.where(row == lane, live_ref[...], 0), axis=1, keepdims=True)
    odd = lax.axis_index("band") % 2
    slot = lax.broadcasted_iota(jnp.int32, (blocks, TABLE), 1)
    x_first = 8 + RB * odd
    i_first = 8 + RB * (1 - odd)
    ids = jnp.where(slot < 8, slot, jnp.where(slot < 8 + RB, slot - 8 + x_first, slot - 8 - RB + i_first))
    ids = jnp.where(slot < 8 + 2 * RB, ids, -1)
    table = table_of(lists_ref[...], live, ids, count, tok)
    table_ref[:TABLE] = table
    past = lax.broadcasted_iota(jnp.int32, (tok - RIM, tok), 0) + RIM >= count
    tail = [jnp.broadcast_to(table[at : at + 1], (BLK, tok)) for at in range(RB, tok // BLK)]
    table_ref[TABLE:] = jnp.where(past, NEG, jnp.concatenate(tail, axis=0))
    for h in range(SPLIT):
        q, k, v, g = (ref[:, cols(h)] for ref in (q_ref, k_ref, v_ref, g_ref))
        top, p = own_exps(nt(k, q), table_ref)
        prod = nt(v, g)
        p_ref[h], prod_ref[h] = p, prod
        stats_ref[h] = rows_of(sums_of(top, p, prod))


def first_kernel(q_ref, g_ref, x_ref, table_ref, stats_ref, p_ref, prod_ref):
    for h in range(SPLIT):
        q, g = q_ref[:, cols(h)], g_ref[:, cols(h)]
        top, p = exps_of(nt(x_ref[:RIM, cols(h)], q), table_ref, 8)
        prod = nt(x_ref[RIM : 2 * RIM, cols(h)], g)
        p_ref[h], prod_ref[h] = p, prod
        stats_ref[h] = rows_of(sums_of(top, p, prod))


def rim_kernel(first, q_ref, g_ref, x_ref, i_ref, table_ref, *refs):
    if first:
        k_ref, v_ref, gx_ref, final_ref, ds_ref, pi_ref, prodi_ref, po_ref, prodo_ref = refs
    else:
        stats_ref, stats_x_ref, px_ref, prodx_ref, gx_ref, final_ref, ds_ref, pi_ref, prodi_ref = refs
    if not first:
        pack_head(q_ref, g_ref, HEADS - SENT, gx_ref)
    heads = range(x_ref.shape[1] // DEPTH)
    returned = len(heads) - (SENT if first else 0)
    parts = []
    for at in heads:
        h = first + at
        q, g = q_ref[:, cols(h)], g_ref[:, cols(h)]
        top, p = exps_of(nt(i_ref[0, :, cols(h)], q), table_ref, 8 + RB)
        prod = nt(i_ref[1, :, cols(h)], g)
        pi_ref[at], prodi_ref[at] = p, prod
        part_i = sums_of(top, p, prod)
        if first:
            top, p = exps_of(nt(x_ref[:RIM, cols(at)], q), table_ref, 8)
            prod = nt(x_ref[RIM : 2 * RIM, cols(at)], g)
            part_x = sums_of(top, p, prod)
            top, po = own_exps(nt(k_ref[:, cols(h)], q), table_ref)
            prodo = nt(v_ref[:, cols(h)], g)
            po_ref[at], prodo_ref[at] = po, prodo
            own = sums_of(top, po, prodo)
        else:
            part_x, p, prod = known(stats_x_ref.at[h]), px_ref[h], prodx_ref[h]
            own = known(stats_ref.at[h])
        parts.append((own, part_i, part_x, p, prod))
    for at, (own, part_i, part_x, p, prod) in zip(heads, parts):
        h = first + at
        q, g = q_ref[:, cols(h)], g_ref[:, cols(h)]
        top, total, raw = merged(merged(own, part_i), part_x)
        inv = jnp.where(total > 0.0, 1.0 / jnp.where(total > 0.0, total, 1.0), 0.0)
        delta = raw * inv
        w, ds = grads_of(p, prod, jnp.exp2(part_x[0] - top) * inv, delta)
        if at < returned:
            gx_ref[:RIM, cols(at)] = nn(ds, q).astype(jnp.bfloat16)
            gx_ref[RIM : 2 * RIM, cols(at)] = nn(w, g).astype(jnp.bfloat16)
        else:
            rows = jnp.concatenate([table_ref[8 : 8 + RB] - top, inv, delta], axis=0)
            begin = 2 * RIM + (at - returned) * STATS
            gx_ref[begin : begin + STATS, : rows.shape[1]] = thirds_of(rows)
        ds_ref[at] = ds
        final_ref[at] = rows_of((jnp.exp2(own[0] - top) * inv, jnp.exp2(part_i[0] - top) * inv, delta))


def inside_kernel(q_ref, g_ref, *refs):
    gi_ref, ds_ref = refs[-2:]
    for h in range(HEADS):
        final_ref, pi_ref, prodi_ref = refs[:3] if h < SPLIT else refs[3:6]
        at = h if h < SPLIT else h - SPLIT
        q, g = q_ref[:, cols(h)], g_ref[:, cols(h)]
        w, ds = grads_of(pi_ref[at], prodi_ref[at], final_ref[at, 1:2], final_ref[at, 2:3])
        gi_ref[0, :, cols(h)] = nn(ds, q).astype(jnp.bfloat16)
        gi_ref[1, :, cols(h)] = nn(w, g).astype(jnp.bfloat16)
        ds_ref[h] = ds


def rest_kernel(q_ref, k_ref, v_ref, g_ref, i_ref, dsi_ref, *refs):
    parts, (_, dq_ref, pk_ref, pv_ref, score_ref, products_ref, dq_buf, sems) = (refs[:5], refs[5:10]), refs[10:]
    x_ref = parts[1][1]
    score_ref[...] = nt(k_ref[:RIM, cols(HEADS - 1)], sent_of(x_ref, 0))
    products_ref[...] = nt(v_ref[:RIM, cols(HEADS - 1)], sent_of(x_ref, 1))
    copies = []
    for h in range(HEADS):
        at = h if h < SPLIT else h - SPLIT
        final_ref, x_ref, dsx_ref, p_ref, prod_ref = parts[0] if h < SPLIT else parts[1]
        q, k, g = (ref[:, cols(h)] for ref in (q_ref, k_ref, g_ref))
        w, ds = grads_of(p_ref[at], prod_ref[at], final_ref[at, 0:1], final_ref[at, 2:3])
        pk_ref[:, cols(h)] = nn(ds, q)
        pv_ref[:, cols(h)] = nn(w, g)
        frame_k = jnp.concatenate([k, x_ref[:RIM, cols(at)], i_ref[0, :, cols(h)]], axis=0)
        dq = tn(frame_k, jnp.concatenate([ds, dsx_ref[at], dsi_ref[h]], axis=0))
        dq_buf[:, cols(h)] = dq.T.astype(jnp.bfloat16)
        if at == SPLIT - 1:
            span = (slice(None), pl.ds((h + 1 - SPLIT) * DEPTH, SPLIT * DEPTH))
            copies.append(pltpu.make_async_copy(dq_buf.at[span], dq_ref.at[span], sems.at[len(copies)]))
            copies[-1].start()
    for copy in copies:
        copy.wait()


def summed(own_ref, lead, gi_ref, slot, h):
    lead = own_ref[:RIM, cols(h)] + (lead + gi_ref[slot, :, cols(h)].astype(jnp.float32))
    return jnp.concatenate([lead, own_ref[RIM:, cols(h)]], axis=0).astype(jnp.bfloat16)


def done_kernel(k_ref, v_ref, pk_ref, pv_ref, gx_ref, gi_ref, dk_ref, dv_ref, score_ref, products_ref):
    for slot, (own, out) in enumerate(((pk_ref, dk_ref), (pv_ref, dv_ref))):
        for h in range(SPLIT):
            lead = gx_ref[slot * RIM : (slot + 1) * RIM, cols(h)].astype(jnp.float32)
            out[:, cols(h)] = summed(own, lead, gi_ref, slot, h)
    score_ref[...] = nt(k_ref[:RIM, cols(HEADS - SENT)], sent_of(gx_ref, 0))
    products_ref[...] = nt(v_ref[:RIM, cols(HEADS - SENT)], sent_of(gx_ref, 1))


def final_kernel(dk_in, dv_in, pk_ref, pv_ref, gx_ref, gi_ref, *refs):
    sent, (dk_ref, dv_ref, dk_buf, dv_buf, sems) = (refs[:3], refs[3:6]), refs[6:]
    heads = HEADS - SPLIT
    early = pl.ds(0, SPLIT * DEPTH)
    late = pl.ds(SPLIT * DEPTH, heads * DEPTH)
    copies = [
        pltpu.make_async_copy(dk_in, dk_ref.at[:, early], sems.at[0]),
        pltpu.make_async_copy(dv_in, dv_ref.at[:, early], sems.at[1]),
        pltpu.make_async_copy(dk_buf, dk_ref.at[:, late], sems.at[2]),
        pltpu.make_async_copy(dv_buf, dv_ref.at[:, late], sems.at[3]),
    ]
    for copy in copies[:2]:
        copy.start()
    returned = heads - SENT
    leads = {}
    for n, (from_ref, score_ref, prod_ref) in enumerate(sent):
        begin = 2 * RIM + n * STATS
        rows = whole_of(gx_ref[begin : begin + STATS, : score_ref.shape[1]].astype(jnp.float32))
        blocks = [jnp.exp2(score_ref[e * BLK : (e + 1) * BLK] * SCALE + rows[e : e + 1]) for e in range(RB)]
        w, ds = grads_of(jnp.concatenate(blocks, axis=0), prod_ref[...], rows[RB : RB + 1], rows[RB + 1 : RB + 2])
        leads[returned + n] = nn(ds, sent_of(from_ref, 0)), nn(w, sent_of(from_ref, 1))
    for slot, (own, buf) in enumerate(((pk_ref, dk_buf), (pv_ref, dv_buf))):
        for at in range(heads):
            if at in leads:
                lead = leads[at][slot]
            else:
                lead = gx_ref[slot * RIM : (slot + 1) * RIM, cols(at)].astype(jnp.float32)
            buf[:, cols(at)] = summed(own, lead, gi_ref, slot, SPLIT + at)
        copies[2 + slot].start()
    for copy in copies:
        copy.wait()


VMEM = pl.BlockSpec(memory_space=pltpu.VMEM)
HBM = pl.BlockSpec(memory_space=pltpu.HBM)
ANY = pl.BlockSpec(memory_space=pl.ANY)


def call(body, name, ins, outs, out_specs, args, scratch=(), alias=None, limit=24):
    return pl.pallas_call(
        body,
        in_specs=ins,
        out_specs=out_specs,
        out_shape=outs,
        scratch_shapes=scratch,
        input_output_aliases=alias or {},
        compiler_params=pltpu.CompilerParams(vmem_limit_bytes=int(limit * MIB)),
        cost_estimate=pl.CostEstimate(flops=WEIGHT[name] * MEGA, bytes_accessed=1000, transcendentals=0),
        name=name,
    )(*args)


def shape(*dims, dtype=jnp.bfloat16):
    return jax.ShapeDtypeStruct(dims, dtype)


def on_device(queries, keys, values, out_grad, band_counts, block_lists, slot_counts):
    tok, width = queries.shape
    f32 = functools.partial(shape, dtype=jnp.float32)
    cuts = ((0, SPLIT), (SPLIT, HEADS))
    part = HEADS - SPLIT
    q, k, v, g = queries, keys, values, out_grad
    lead_a = call(
        load_kernel,
        "load_bands",
        [HBM] * 2,
        shape(2 * RIM, SPLIT * DEPTH),
        VMEM,
        (k, v),
        [pltpu.SemaphoreType.DMA((2,))],
        limit=LOAD_LIMIT,
    )
    lead_b = call(pack_kernel, "pack_leads", [VMEM] * 4, shape(2 * RIM + tok // PIECES, part * DEPTH), VMEM, (k, v, q, g))
    x_a, x_b = swap_across(lead_a), swap_across(lead_b)
    lead_i = call(inside_pack_kernel, "pack_inside", [VMEM] * 2 + [ANY], shape(2, RIM, width), VMEM, (k, v, lead_b))
    i = swap_inside(lead_i)
    table, stats, p, prod = call(
        own_kernel,
        "own_stats",
        [VMEM] * 7,
        [f32(TABLE + tok - RIM, tok), f32(SPLIT, 8, tok), f32(SPLIT, tok, tok), f32(SPLIT, tok, tok)],
        [VMEM] * 4,
        (band_counts[:, None], slot_counts[None], block_lists, q, k, v, g),
    )
    stats_x, px, prodx = call(
        first_kernel,
        "first_stats",
        [VMEM] * 4,
        [f32(SPLIT, 8, tok), f32(SPLIT, RIM, tok), f32(SPLIT, RIM, tok)],
        [VMEM] * 3,
        (q, g, x_a, table),
    )

    def rim(first, x, *more):
        heads = x.shape[1] // DEPTH
        gx = (2 * RIM + SENT * STATS, (heads - SENT) * DEPTH) if first else (x.shape[0] + tok // PIECES, x.shape[1])
        return call(
            functools.partial(rim_kernel, first),
            "rim_grads",
            [VMEM] * (5 + len(more)),
            [shape(*gx), f32(heads, 8, tok), shape(heads, RIM, tok), f32(heads, RIM, tok), f32(heads, RIM, tok)]
            + ([f32(heads, tok, tok)] * 2 if first else []),
            [VMEM] * (7 if first else 5),
            (q, g, x, i, table) + more,
        )

    gx_a, final_a, dsx_a, *inside_a = rim(0, x_a, stats, stats_x, px, prodx)
    gx_a = swap_across(gx_a)
    gx_b, final_b, dsx_b, *inside_b, p_b, prod_b = rim(SPLIT, x_b, k, v)
    gx_b = swap_across(gx_b)
    gi, ds_i = call(
        inside_kernel,
        "inside_grads",
        [VMEM] * 8,
        [shape(2, RIM, width), shape(HEADS, RIM, tok)],
        [VMEM] * 2,
        (q, g, final_a, *inside_a, final_b, *inside_b),
    )
    gi = swap_inside(gi)

    dq, pk, pv, *last = call(
        rest_kernel,
        "rest_grads",
        [VMEM] * 16 + [ANY],
        [shape(tok, width), f32(tok, width), f32(tok, width), f32(RIM, tok), f32(RIM, tok)],
        [ANY] + [VMEM] * 4,
        (q, k, v, g, i, ds_i, final_a, x_a, dsx_a, p, prod, final_b, x_b, dsx_b, p_b, prod_b, gx_a),
        [pltpu.VMEM((tok, width), jnp.bfloat16), pltpu.SemaphoreType.DMA((2,))],
    )
    dk_a, dv_a, *other = call(
        done_kernel,
        "done_grads",
        [VMEM] * 6,
        [shape(tok, SPLIT * DEPTH)] * 2 + [f32(RIM, tok)] * 2,
        [VMEM] * 4,
        (k, v, pk, pv, gx_a, gi),
    )
    dk, dv = call(
        final_kernel,
        "final_sums",
        [VMEM] * 12,
        [shape(tok, width)] * 2,
        [ANY] * 2,
        (dk_a, dv_a, pk, pv, gx_b, gi, gx_a, *other, x_b, *last),
        [pltpu.VMEM((tok, part * DEPTH), jnp.bfloat16)] * 2 + [pltpu.SemaphoreType.DMA((4,))],
    )
    return dq, dk, dv


def solution(mesh):
    placed = P(("member", "band"), None)
    flat = P(("member", "band"))
    return jax.shard_map(
        on_device,
        mesh=mesh,
        in_specs=(placed, placed, placed, placed, flat, placed, flat),
        out_specs=(placed, placed, placed),
        check_vma=False,
    )
```
